32 devices in a mesh: parts: 2 (over x), ref: 16 (over z, y, core).
Axes of the slice: x: 2, y: 2, z: 4, core: 2. Of those that a mesh axis runs over, the one named last changes fastest.
Arguments:
- queries: float32 [4096, 128], P('parts'), parts along dimension 0, may hold values from -15 to 15, as said below
- references: float32 [65536, 128], P(('parts', 'ref')), parts along dimension 0, may hold values from -15 to 15
- query_ids: int32 [4096], P('parts'), parts along dimension 0, may hold values from 0 to 32767, as said below
- spread: float32 [128], replicated, may hold values from 0.5 to 2
- cotangent: float32 [4096], P('parts'), parts along dimension 0, may hold values from -4 to 4
Outputs:
- query_grad: float32 [4096, 128], P(('parts', 'ref')), parts along dimension 0
- reference_grad: float32 [65536, 128], P(('parts', 'ref')), parts along dimension 0
- spread_grad: float32 [256], P('parts'), parts along dimension 0
The draws below stay inside these ranges and needn't reach their ends.
There are 2 independent parts, one for each index of `parts`. The reference program is written for one: setup_inputs(seed, part) draws one part's arguments, and reference() takes and returns one part's arrays. A program takes and returns all parts, laid end to end along the dimension named above; an argument that names none is the same for every part. Nothing has to cross between parts.
Inputs may be any that keep to these rules, and one draw needn't show every extreme that they name: `query_ids`: distinct rows of the references; query i is the reference row query_ids_i. `queries`: row i equals row query_ids_i of references.
All inputs are finite; a program needn't handle non-finite values.
Results may differ from the reference program's by a relative error of at most 0.014.
Values sent between devices are 32-bit elements; how exact they have to be, the bound alone decides.
A program may use at most 64 MiB of HBM per device.

```python
import math
import jax
import jax.numpy as jnp
from jax import lax

F = 128
NQ = 2048
R_DEV = 2048
NR = 32768
N_REF = 16


def shared_draw(key):
    key_z = jax.random.fold_in(key, 11)
    key_s = jax.random.fold_in(key, 12)
    key_i = jax.random.fold_in(key, 13)
    values = jnp.clip(jax.random.normal(key_z, (NR, F), jnp.float32), -5.0, 5.0)
    scales = jnp.exp(jax.random.uniform(key_s, (NR, 1), jnp.float32, math.log(0.3), math.log(3.0)))
    rows = values * scales
    picked = jax.random.permutation(key_i, NR)[:NQ].astype(jnp.int32)
    return (rows, picked)


def draw_references(key, part):
    rows, picked = shared_draw(key)
    return rows


def draw_queries(key, part):
    rows, picked = shared_draw(key)
    return rows[picked]


def draw_query_ids(key, part):
    rows, picked = shared_draw(key)
    return picked


def gaussian(rng, shape, deviation, reach, held_as=jnp.bfloat16):
    return jnp.clip(deviation * jax.random.normal(rng, shape, jnp.float32), -reach, reach).astype(held_as)


def setup_inputs(seed: int = 0, part: int = 0) -> dict:
    splits = jax.random.split(jax.random.key(seed), 6)
    own_keys = jax.random.split(jax.random.fold_in(splits[5], part), 6)
    return {
        "queries": draw_queries(jax.random.fold_in(jax.random.fold_in(splits[5], part), 71), part),
        "references": draw_references(jax.random.fold_in(jax.random.fold_in(splits[5], part), 71), part),
        "query_ids": draw_query_ids(jax.random.fold_in(jax.random.fold_in(splits[5], part), 71), part),
        "spread": jnp.clip(jnp.exp(jax.random.uniform(splits[3], (F,), jnp.float32, math.log(0.5), math.log(2.0))), 0.5, 2.0),
        "cotangent": gaussian(own_keys[4], (NQ,), 1.0, 4.0, jnp.float32),
    }


def reference(queries, references, query_ids, spread, cotangent):
    inv = 1.0 / (spread * spread)
    scaled = queries * inv
    qnorm = jnp.sum(queries * queries * inv, axis=1)
    ref_blocks = references.reshape(N_REF, R_DEV, F)
    starts = (jnp.arange(N_REF, dtype=jnp.int32) * R_DEV).astype(jnp.int32)
    columns = jnp.arange(R_DEV, dtype=jnp.int32)

    def block_score(block, start):
        cross = jnp.dot(scaled, block.T, precision=lax.Precision.HIGHEST, preferred_element_type=jnp.float32)
        rnorm = jnp.sum(block * block * inv, axis=1)
        score = cross - 0.5 * qnorm[:, None] - 0.5 * rnorm[None, :]
        self_mask = (query_ids - start)[:, None] == columns[None, :]
        return jnp.where(self_mask, -jnp.inf, score), self_mask

    def forward(carry, items):
        peak_now, total_now = carry
        block, start = items
        score, self_mask = block_score(block, start)
        new_peak = jnp.maximum(peak_now, jnp.max(score, axis=1))
        new_total = total_now * jnp.exp(peak_now - new_peak) + jnp.sum(jnp.exp(score - new_peak[:, None]), axis=1)
        return (new_peak, new_total), None

    init = (jnp.full((NQ,), -jnp.inf, jnp.float32), jnp.zeros((NQ,), jnp.float32))
    (peak, total), unused = lax.scan(forward, init, (ref_blocks, starts))
    query_low = queries.astype(jnp.bfloat16)

    def backward(pulled, items):
        block, start = items
        score, self_mask = block_score(block, start)
        weight = jnp.where(self_mask, 0.0, cotangent[:, None] * jnp.exp(score - peak[:, None]) / total[:, None]).astype(jnp.bfloat16)
        pulled = pulled + jnp.dot(weight, block.astype(jnp.bfloat16), preferred_element_type=jnp.float32)
        pushed = jnp.dot(weight.T, query_low, preferred_element_type=jnp.float32)
        column = jnp.sum(weight.astype(jnp.float32), axis=0)
        rgrad = (pushed - block * column[:, None]) * inv
        return pulled, (rgrad, jnp.sum(block * rgrad, axis=0))

    pulled, (rgrads, rdr) = lax.scan(backward, jnp.zeros((NQ, F), jnp.float32), (ref_blocks, starts))
    query_grad = (pulled - queries * cotangent[:, None]) * inv
    reference_grad = rgrads.reshape(NR, F)
    summed = jnp.sum(queries * query_grad, axis=0) + jnp.sum(rdr, axis=0)
    spread_grad = -summed / spread - jnp.sum(cotangent) / spread
    return query_grad, reference_grad, spread_grad
```

```python
import functools
import math

import jax
import jax.numpy as jnp
from jax import lax
from jax.experimental import pallas as pl
from jax.experimental.pallas import tpu as pltpu
from jax.sharding import PartitionSpec as P

LOG2E = math.log2(math.e)
TILE = 256
CHUNK = 512


def split3(x):
    a = x.astype(jnp.bfloat16).astype(jnp.float32)
    b = (x - a).astype(jnp.bfloat16).astype(jnp.float32)
    c = (x - a - b).astype(jnp.bfloat16).astype(jnp.float32)
    return a, b, c


def kernel(
    n, q_ref, r_ref, ids_ref, sp_ref, cot_ref, qg_ref, rg_ref, sg_ref,
    qat, ra, rta, pt, s0, s1, m_ref, ut, cq, qt, xt, lse, lse_rx, term, term_rx, *rest
):
    steps = n.bit_length() - 1
    acc = rest[:steps]
    got = rest[steps:2 * steps]
    ls_send, ls_recv, tm_send, tm_recv, rs_send, rs_recv = rest[2 * steps:]
    nq, nf = q_ref.shape
    nr = r_ref.shape[0]
    own = nq // n
    f32, bf16 = jnp.float32, jnp.bfloat16
    me = lax.axis_index("ref")

    def peer_of(k):
        return lax.rem(me + k, n)

    barrier = pltpu.get_barrier_semaphore()

    def greet(k, carry):
        pl.semaphore_signal(
            barrier, inc=1, device_id={"ref": peer_of(k)}, device_id_type=pl.DeviceIdType.MESH
        )
        return carry

    lax.fori_loop(1, n, greet, 0)

    sp = sp_ref[...]
    inv = 1.0 / (sp * sp)
    inv_col = jnp.transpose(jnp.broadcast_to(inv, (8, nf)))[:, :1]
    for a in range(0, nq, TILE):
        rows = slice(a, a + TILE)
        q_t = jnp.transpose(q_ref[rows, :])
        qt[:, rows] = q_t
        scaled = q_t * (inv_col * LOG2E)
        high = scaled.astype(bf16)
        low = (scaled - high.astype(f32)).astype(bf16)
        qat[0:nf, rows] = high
        qat[nf:2 * nf, rows] = low
        qat[2 * nf:3 * nf, rows] = high
        norm = -0.5 * jnp.sum(q_t * scaled, axis=0, keepdims=True)
        n1, n2, n3 = split3(norm)
        place = lax.broadcasted_iota(jnp.int32, (nf, TILE), 0)
        ext = jnp.where(place < 6, 1.0, 0.0)
        ext = jnp.where(place == 0, n1, ext)
        ext = jnp.where(place == 1, n2, ext)
        ext = jnp.where(place == 2, n3, ext)
        qat[3 * nf:4 * nf, rows] = ext.astype(bf16)
    for a in range(0, nr, TILE):
        rows = slice(a, a + TILE)
        r = r_ref[rows, :]
        high = r.astype(bf16)
        low = (r - high.astype(f32)).astype(bf16)
        ra[rows, 0:nf] = high
        ra[rows, nf:2 * nf] = high
        ra[rows, 2 * nf:3 * nf] = low
        norm = -0.5 * LOG2E * jnp.sum(r * r * inv, axis=1, keepdims=True)
        n1, n2, n3 = split3(norm)
        place = lax.broadcasted_iota(jnp.int32, (TILE, nf), 1)
        ext = jnp.where(place < 6, 1.0, 0.0)
        ext = jnp.where(place == 3, n1, ext)
        ext = jnp.where(place == 4, n2, ext)
        ext = jnp.where(place == 5, n3, ext)
        ra[rows, 3 * nf:4 * nf] = ext.astype(bf16)
        rta[0:nf, rows] = jnp.transpose(r).astype(bf16)
    rta[nf:nf + 16, :] = jnp.ones((16, nr), bf16)

    start = me * nr

    def at(t):
        return pl.ds(pl.multiple_of(t * TILE, TILE), TILE)

    def score(t, s_ref, a, best):
        s = jnp.dot(ra[a:a + CHUNK, :], qat[:, at(t)], preferred_element_type=f32)
        local = ids_ref[:, at(t)] - (start + a)
        hit = lax.broadcasted_iota(jnp.int32, (CHUNK, TILE), 0) == local
        s = jnp.where(hit, -jnp.inf, s)
        s_ref[a:a + CHUNK, :] = s
        top = jnp.max(s, axis=0, keepdims=True)
        return top if best is None else jnp.maximum(best, top)

    def weigh(t, s_ref, a, peak, total):
        p = jnp.exp2(s_ref[a:a + CHUNK, :] - peak).astype(bf16)
        pt[a:a + CHUNK, at(t)] = p
        part = jnp.dot(rta[:, a:a + CHUNK], p, preferred_element_type=f32)
        return part if total is None else total + part

    def stage(ahead, s_ahead, t, s_now):
        best, total = None, None
        peak = None if t is None else m_ref[:, at(t)]
        for a in range(0, nr, CHUNK):
            if ahead is not None:
                best = score(ahead, s_ahead, a, best)
            if t is not None:
                total = weigh(t, s_now, a, peak, total)
        if ahead is not None:
            m_ref[:, at(ahead)] = best
        if t is not None:
            ut[:, at(t)] = total

    tiles = nq // TILE
    stage(0, s0, None, None)

    def pair(t, carry):
        stage(2 * t + 1, s1, 2 * t, s0)
        stage(2 * t + 2, s0, 2 * t + 1, s1)
        return carry

    lax.fori_loop(0, tiles // 2 - 1, pair, 0)
    stage(tiles - 1, s1, tiles - 2, s0)
    stage(None, None, tiles - 1, s1)

    peak = m_ref[...]
    mine = peak + jnp.log(ut[nf:nf + 1, :]) * LOG2E
    lse[...] = mine
    pl.semaphore_wait(barrier, n - 1)

    def all_to(src, dst, send, recv):
        def copy(k):
            return pltpu.make_async_remote_copy(
                src_ref=src, dst_ref=dst.at[k - 1], send_sem=send.at[k - 1], recv_sem=recv.at[k - 1],
                device_id={"ref": peer_of(k)}, device_id_type=pl.DeviceIdType.MESH,
            )

        def begin(k, carry):
            copy(k).start()
            return carry

        def end(k, carry):
            copy(k).wait()
            return carry

        return (lambda: lax.fori_loop(1, n, begin, 0)), (lambda: lax.fori_loop(1, n, end, 0))

    lse_start, lse_wait = all_to(lse, lse_rx, ls_send, ls_recv)
    lse_start()
    cot = cot_ref[...]
    cot_q = jnp.zeros((1, nf), f32)
    for a in range(0, nq, TILE):
        rows = slice(a, a + TILE)
        part = jnp.transpose(qt[:, rows] * cot[:, rows])
        cq[rows, :] = part
        cot_q = cot_q + jnp.sum(part * q_ref[rows, :], axis=0, keepdims=True)
    lse_wait()
    every = lse_rx[...]
    top = jnp.maximum(mine, jnp.max(every, axis=0))
    whole = jnp.exp2(mine - top) + jnp.sum(jnp.exp2(every - top[None]), axis=0)
    coef = cot * jnp.exp2(peak - top) / whole

    terms = jnp.zeros((1, nf), f32)
    for a in range(0, nq, TILE):
        rows = slice(a, a + TILE)
        part = jnp.transpose(ut[0:nf, rows] * coef[:, rows])
        terms = terms + jnp.sum(part * q_ref[rows, :], axis=0, keepdims=True)
        if own >= TILE:
            acc[0][a // (2 * own), (a // own) % 2, a % own:a % own + TILE, :] = part
        else:
            for b in range(0, TILE, own):
                k = (a + b) // own
                acc[0][k // 2, k % 2] = part[b:b + own]

    def halving(b):
        size = 2 ** b
        bit = lax.rem(me // size, 2)
        partner = me + (1 - 2 * bit) * size
        return bit, pltpu.make_async_remote_copy(
            src_ref=acc[b].at[:, 1 - bit], dst_ref=got[b], send_sem=rs_send.at[b], recv_sem=rs_recv.at[b],
            device_id={"ref": partner}, device_id_type=pl.DeviceIdType.MESH,
        )

    def settle(b):
        bit, copy = halving(b)
        copy.wait()
        kept = n // 2 ** (b + 1)
        if b + 1 < steps:
            for k in range(kept):
                acc[b + 1][k // 2, k % 2] = acc[b][k, bit] + got[b][k]
            halving(b + 1)[1].start()
            return None
        return acc[b][0, bit] + got[b][0]

    halving(0)[1].start()

    row = lax.broadcasted_iota(jnp.int32, (nf, TILE), 0)
    for a in range(0, nq, TILE):
        rows = slice(a, a + TILE)
        c = coef[:, rows]
        c1, c2, _ = split3(c)
        extra = jnp.where(row == 0, c1, jnp.where(row == 1, c2, 0.0))
        xt[rows, 0:nf] = jnp.transpose(qt[:, rows] * c).astype(bf16)
        xt[rows, nf:2 * nf] = jnp.transpose(extra).astype(bf16)
    terms = terms * inv
    done = 0
    pulled = None
    chunks = nr // CHUNK
    for i in range(chunks):
        rows = slice(i * CHUNK, (i + 1) * CHUNK)
        both = jnp.dot(pt[rows, :], xt[...], preferred_element_type=f32)
        r = r_ref[rows, :]
        column = both[:, nf:nf + 1] + both[:, nf + 1:nf + 2]
        grad = (both[:, 0:nf] - r * column) * inv
        rg_ref[rows, :] = grad
        terms = terms + jnp.sum(r * grad, axis=0, keepdims=True)
        if i == 0:
            settle(0)
            done = 1
    term[...] = terms
    term_start, term_wait = all_to(term, term_rx, tm_send, tm_recv)
    term_start()
    for b in range(done, steps):
        pulled = settle(b)
    mine_rows = pl.ds(pl.multiple_of(me * own, own), own)
    qg_ref[...] = (pulled - cq[mine_rows, :]) * inv
    term_wait()
    summed = terms + jnp.sum(term_rx[...], axis=0) - cot_q * inv
    sg_ref[...] = -summed / sp - jnp.sum(cot, axis=1, keepdims=True) / sp


def on_device(n, queries, references, query_ids, spread, cotangent):
    nq, nf = queries.shape
    nr = references.shape[0]
    own = nq // n
    steps = n.bit_length() - 1
    f32, bf16 = jnp.float32, jnp.bfloat16
    halves = [n // 2 ** (b + 1) for b in range(steps)]
    scratch = [
        pltpu.VMEM((4 * nf, nq), bf16),
        pltpu.VMEM((nr, 4 * nf), bf16),
        pltpu.VMEM((nf + 16, nr), bf16),
        pltpu.VMEM((nr, nq), bf16),
        pltpu.VMEM((nr, TILE), f32),
        pltpu.VMEM((nr, TILE), f32),
        pltpu.VMEM((1, nq), f32),
        pltpu.VMEM((nf + 16, nq), f32),
        pltpu.VMEM((nq, nf), f32),
        pltpu.VMEM((nf, nq), f32),
        pltpu.VMEM((nq, 2 * nf), bf16),
        pltpu.VMEM((1, nq), f32),
        pltpu.VMEM((n - 1, 1, nq), f32),
        pltpu.VMEM((1, nf), f32),
        pltpu.VMEM((n - 1, 1, nf), f32),
    ]
    scratch += [pltpu.VMEM((h, 2, own, nf), f32) for h in halves]
    scratch += [pltpu.VMEM((h, own, nf), f32) for h in halves]
    scratch += [pltpu.SemaphoreType.DMA((n - 1,))] * 4
    scratch += [pltpu.SemaphoreType.DMA((steps,))] * 2
    vmem = pl.BlockSpec(memory_space=pltpu.VMEM)
    query_grad, reference_grad, spread_grad = pl.pallas_call(
        functools.partial(kernel, n),
        out_shape=(
            jax.ShapeDtypeStruct((own, nf), f32),
            jax.ShapeDtypeStruct((nr, nf), f32),
            jax.ShapeDtypeStruct((1, nf), f32),
        ),
        in_specs=[vmem] * 5,
        out_specs=(vmem, vmem, vmem),
        scratch_shapes=scratch,
        compiler_params=pltpu.CompilerParams(
            collective_id=0, has_side_effects=True, vmem_limit_bytes=52 * 2 ** 20
        ),
    )(queries, references, query_ids[None, :], spread[None, :], cotangent[None, :])
    return query_grad, reference_grad, spread_grad[0]


def solution(mesh):
    placed = (P("parts", None), P(("parts", "ref"), None), P("parts"), P(), P("parts"))
    return jax.shard_map(
        functools.partial(on_device, mesh.shape["ref"]),
        mesh=mesh,
        in_specs=placed,
        out_specs=(P(("parts", "ref"), None), P(("parts", "ref"), None), P("parts")),
        check_vma=False,
    )
```

```python
import functools
import math

import jax
import jax.numpy as jnp
from jax import lax
from jax.experimental import pallas as pl
from jax.experimental.pallas import tpu as pltpu
from jax.sharding import PartitionSpec as P

LOG2E = math.log2(math.e)
TILE = 256
CHUNK = 512


def split3(x):
    a = x.astype(jnp.bfloat16).astype(jnp.float32)
    b = (x - a).astype(jnp.bfloat16).astype(jnp.float32)
    c = (x - a - b).astype(jnp.bfloat16).astype(jnp.float32)
    return a, b, c


def plan(n):
    last = n.bit_length() - 2
    mid = (last + 1) // 2
    first = list(range(last))
    second = [0] + [b for b in range(mid, last)] + [b for b in range(1, mid)]
    return last, (first, second)


def layouts(n):
    last, orders = plan(n)
    shapes = []
    for order in orders:
        left = list(range(last))
        group = []
        for b in order:
            place = left.index(b)
            group.append((2 ** (len(left) - 1 - place), 2, 2 ** place))
            left.remove(b)
        shapes.append(group)
    return shapes


def kernel(
    n, q_ref, r_ref, ids_hbm, sp_hbm, cot_hbm, qg_ref, rg_hbm, sg_ref,
    rg_ref, rg_sem, ids_ref, sp_ref, cot_ref, in_sem,
    qat, ra, rta, pt, s0, s1, m_ref, ut, cq, qt, xt, push, fin, fin_got, term, term_rx, *rest
):
    last, orders = plan(n)
    shapes = layouts(n)
    rest = list(rest)
    lse = [rest.pop(0) for _ in range(2)]
    lse_rx = [rest.pop(0) for _ in range(2)]
    acc = [[rest.pop(0) for _ in range(last)] for _ in range(2)]
    got = [[rest.pop(0) for _ in range(last)] for _ in range(2)]
    ls_send, ls_recv = rest[0:2], rest[2:4]
    rs_send, rs_recv = rest[4:6], rest[6:8]
    tm_send, tm_recv, fin_sem = rest[8:]
    nq, nf = q_ref.shape
    nr = r_ref.shape[0]
    own = nq // n
    half = nq // 2
    f32, bf16 = jnp.float32, jnp.bfloat16
    me = lax.axis_index("ref")

    loads = [
        pltpu.make_async_copy(src, dst, in_sem.at[i])
        for i, (src, dst) in enumerate(((ids_hbm, ids_ref), (sp_hbm, sp_ref), (cot_hbm, cot_ref)))
    ]
    for load in loads:
        load.start()

    def peer_of(k):
        return lax.rem(me + k, n)

    barrier = pltpu.get_barrier_semaphore()

    def greet(k, carry):
        pl.semaphore_signal(
            barrier, inc=1, device_id={"ref": peer_of(k)}, device_id_type=pl.DeviceIdType.MESH
        )
        return carry

    lax.fori_loop(1, n, greet, 0)
    for load in loads:
        load.wait()

    sp = sp_ref[...]
    inv = 1.0 / (sp * sp)
    inv_col = jnp.transpose(jnp.broadcast_to(inv, (8, nf)))[:, :1]
    for a in range(0, nq, TILE):
        rows = slice(a, a + TILE)
        q_t = jnp.transpose(q_ref[rows, :])
        qt[:, rows] = q_t
        scaled = q_t * (inv_col * LOG2E)
        high = scaled.astype(bf16)
        low = (scaled - high.astype(f32)).astype(bf16)
        qat[0:nf, rows] = high
        qat[nf:2 * nf, rows] = low
        qat[2 * nf:3 * nf, rows] = high
        norm = -0.5 * jnp.sum(q_t * scaled, axis=0, keepdims=True)
        n1, n2, n3 = split3(norm)
        place = lax.broadcasted_iota(jnp.int32, (nf, TILE), 0)
        ext = jnp.where(place < 6, 1.0, 0.0)
        ext = jnp.where(place == 0, n1, ext)
        ext = jnp.where(place == 1, n2, ext)
        ext = jnp.where(place == 2, n3, ext)
        qat[3 * nf:4 * nf, rows] = ext.astype(bf16)
    for a in range(0, nr, TILE):
        rows = slice(a, a + TILE)
        r = r_ref[rows, :]
        high = r.astype(bf16)
        low = (r - high.astype(f32)).astype(bf16)
        ra[rows, 0:nf] = high
        ra[rows, nf:2 * nf] = high
        ra[rows, 2 * nf:3 * nf] = low
        norm = -0.5 * LOG2E * jnp.sum(r * r * inv, axis=1, keepdims=True)
        n1, n2, n3 = split3(norm)
        place = lax.broadcasted_iota(jnp.int32, (TILE, nf), 1)
        ext = jnp.where(place < 6, 1.0, 0.0)
        ext = jnp.where(place == 3, n1, ext)
        ext = jnp.where(place == 4, n2, ext)
        ext = jnp.where(place == 5, n3, ext)
        ra[rows, 3 * nf:4 * nf] = ext.astype(bf16)
        rta[0:nf, rows] = jnp.transpose(r).astype(bf16)
    rta[nf:nf + 16, :] = jnp.ones((16, nr), bf16)

    start = me * nr

    def at(t):
        return pl.ds(pl.multiple_of(t * TILE, TILE), TILE)

    def score(t, s_ref, a, best):
        s = jnp.dot(ra[a:a + CHUNK, :], qat[:, at(t)], preferred_element_type=f32)
        local = ids_ref[:, at(t)] - (start + a)
        hit = lax.broadcasted_iota(jnp.int32, (CHUNK, TILE), 0) == local
        s = jnp.where(hit, -jnp.inf, s)
        s_ref[a:a + CHUNK, :] = s
        top = jnp.max(s, axis=0, keepdims=True)
        return top if best is None else jnp.maximum(best, top)

    def weigh(t, s_ref, a, peak, total):
        p = jnp.exp2(s_ref[a:a + CHUNK, :] - peak).astype(bf16)
        pt[a:a + CHUNK, at(t)] = p
        part = jnp.dot(rta[:, a:a + CHUNK], p, preferred_element_type=f32)
        return part if total is None else total + part

    def stage(ahead, s_ahead, t, s_now):
        best, total = None, None
        peak = None if t is None else m_ref[:, at(t)]
        for a in range(0, nr, CHUNK):
            if ahead is not None:
                best = score(ahead, s_ahead, a, best)
            if t is not None:
                total = weigh(t, s_now, a, peak, total)
        if ahead is not None:
            m_ref[:, at(ahead)] = best
        if t is not None:
            ut[:, at(t)] = total

    def all_to(src, dst, send, recv):
        def copy(k):
            return pltpu.make_async_remote_copy(
                src_ref=src, dst_ref=dst.at[k - 1], send_sem=send.at[k - 1], recv_sem=recv.at[k - 1],
                device_id={"ref": peer_of(k)}, device_id_type=pl.DeviceIdType.MESH,
            )

        def begin(k, carry):
            copy(k).start()
            return carry

        def end(k, carry):
            copy(k).wait()
            return carry

        return (lambda: lax.fori_loop(1, n, begin, 0)), (lambda: lax.fori_loop(1, n, end, 0))

    def spread_lse(g):
        cols = slice(g * half, (g + 1) * half)
        lse[g][...] = m_ref[:, cols] + jnp.log(ut[nf:nf + 1, cols]) * LOG2E
        all_to(lse[g], lse_rx[g], ls_send[g], ls_recv[g])[0]()

    def coefficients(g):
        cols = slice(g * half, (g + 1) * half)
        all_to(lse[g], lse_rx[g], ls_send[g], ls_recv[g])[1]()
        every = lse_rx[g][...]
        mine = lse[g][...]
        top = jnp.maximum(mine, jnp.max(every, axis=0))
        whole = jnp.exp2(mine - top) + jnp.sum(jnp.exp2(every - top[None]), axis=0)
        return cot_ref[:, cols] * jnp.exp2(m_ref[:, cols] - top) / whole

    def halving(g, i):
        size = 2 ** orders[g][i]
        bit = lax.rem(me // size, 2)
        return bit, pltpu.make_async_remote_copy(
            src_ref=acc[g][i].at[:, 1 - bit], dst_ref=got[g][i],
            send_sem=rs_send[g].at[i], recv_sem=rs_recv[g].at[i],
            device_id={"ref": me + (1 - 2 * bit) * size}, device_id_type=pl.DeviceIdType.MESH,
        )

    top_bit = lax.rem(me // (n // 2), 2)
    final = pltpu.make_async_remote_copy(
        src_ref=fin.at[1 - top_bit], dst_ref=fin_got, send_sem=fin_sem.at[0], recv_sem=fin_sem.at[1],
        device_id={"ref": me + (1 - 2 * top_bit) * (n // 2)}, device_id_type=pl.DeviceIdType.MESH,
    )

    def place_block(ref, shape, k, value):
        low = shape[2]
        ref[k // (2 * low), (k // low) % 2, k % low] = value

    def pull(g, coef):
        terms = jnp.zeros((1, nf), f32)
        for a in range(0, half, TILE):
            rows = slice(g * half + a, g * half + a + TILE)
            part = jnp.transpose(ut[0:nf, rows] * coef[:, a:a + TILE])
            terms = terms + jnp.sum(part * q_ref[rows, :], axis=0, keepdims=True)
            for b in range(0, TILE, own):
                place_block(acc[g][0], shapes[g][0], (a + b) // own, part[b:b + own])
        halving(g, 0)[1].start()
        return terms

    def settle(g, i):
        bit, copy = halving(g, i)
        copy.wait()
        high, _, low = shapes[g][i]
        for k in range(high * low):
            value = acc[g][i][k // low, bit, k % low] + got[g][i][k // low, k % low]
            if i + 1 < last:
                place_block(acc[g][i + 1], shapes[g][i + 1], k, value)
            else:
                fin[g] = value
        if i + 1 < last:
            halving(g, i + 1)[1].start()
        else:
            @pl.when(top_bit != g)
            def _():
                final.start()

    row = lax.broadcasted_iota(jnp.int32, (nf, TILE), 0)

    def scale_queries(g, coef):
        for a in range(0, half, TILE):
            rows = slice(g * half + a, g * half + a + TILE)
            c = coef[:, a:a + TILE]
            c1, c2, _ = split3(c)
            extra = jnp.where(row == 0, c1, jnp.where(row == 1, c2, 0.0))
            xt[rows, 0:nf] = jnp.transpose(qt[:, rows] * c).astype(bf16)
            xt[rows, nf:2 * nf] = jnp.transpose(extra).astype(bf16)

    def pushed(g, i):
        rows = slice(i * CHUNK, (i + 1) * CHUNK)
        cols = slice(g * half, (g + 1) * half)
        return jnp.dot(pt[rows, cols], xt[cols, :], preferred_element_type=f32)

    stores = [
        pltpu.make_async_copy(
            rg_ref.at[pl.ds(i * CHUNK, CHUNK)], rg_hbm.at[pl.ds(i * CHUNK, CHUNK)], rg_sem.at[i]
        )
        for i in range(nr // CHUNK)
    ]

    def finish(i, terms):
        rows = slice(i * CHUNK, (i + 1) * CHUNK)
        both = push[rows, :] + pushed(1, i)
        r = r_ref[rows, :]
        column = both[:, nf:nf + 1] + both[:, nf + 1:nf + 2]
        grad = (both[:, 0:nf] - r * column) * inv
        rg_ref[rows, :] = grad
        stores[i].start()
        return terms + jnp.sum(r * grad, axis=0, keepdims=True)

    tiles = nq // TILE
    chunks = nr // CHUNK
    stage(0, s0, None, None)

    def pair(t, carry):
        stage(2 * t + 1, s1, 2 * t, s0)
        stage(2 * t + 2, s0, 2 * t + 1, s1)
        return carry

    lax.fori_loop(0, tiles // 4, pair, 0)
    pl.semaphore_wait(barrier, n - 1)
    spread_lse(0)
    lax.fori_loop(tiles // 4, tiles // 2 - 1, pair, 0)
    coef = coefficients(0)
    terms = pull(0, coef)
    stage(tiles - 1, s1, tiles - 2, s0)
    settle(0, 0)
    stage(None, None, tiles - 1, s1)
    spread_lse(1)

    scale_queries(0, coef)
    for i in range(chunks):
        push[i * CHUNK:(i + 1) * CHUNK, :] = pushed(0, i)
    settle(0, 1)
    coef = coefficients(1)
    terms = (terms + pull(1, coef)) * inv
    scale_queries(1, coef)
    terms = finish(0, terms)
    settle(1, 0)
    for i in range(1, chunks):
        terms = finish(i, terms)
    term[...] = terms
    term_start, term_wait = all_to(term, term_rx, tm_send, tm_recv)
    term_start()
    for i in range(2, last):
        settle(0, i)
    for i in range(1, last):
        settle(1, i)
    cot_q = jnp.zeros((1, nf), f32)
    for a in range(0, nq, TILE):
        rows = slice(a, a + TILE)
        part = jnp.transpose(qt[:, rows] * cot_ref[:, rows])
        cq[rows, :] = part
        cot_q = cot_q + jnp.sum(part * q_ref[rows, :], axis=0, keepdims=True)
    for store in stores:
        store.wait()
    term_wait()
    summed = terms + jnp.sum(term_rx[...], axis=0) - cot_q * inv
    sg_ref[...] = -summed / sp - jnp.sum(cot_ref[...], axis=1, keepdims=True) / sp
    mine_rows = pl.ds(pl.multiple_of(me * own, own), own)
    final.wait()
    qg_ref[...] = (fin[top_bit] + fin_got[...] - cq[mine_rows, :]) * inv


def hand_out(*refs):
    sem = refs[-1]
    copies = [pltpu.make_async_copy(refs[i], refs[3 + i], sem.at[i]) for i in range(3)]
    for copy in copies:
        copy.start()
    for copy in copies:
        copy.wait()


def on_device(n, queries, references, query_ids, spread, cotangent):
    nq, nf = queries.shape
    nr = references.shape[0]
    own = nq // n
    half = nq // 2
    f32, bf16 = jnp.float32, jnp.bfloat16
    last, _ = plan(n)
    shapes = layouts(n)
    dma = pltpu.SemaphoreType.DMA
    scratch = [
        pltpu.VMEM((nr, nf), f32),
        dma((nr // CHUNK,)),
        pltpu.VMEM((1, nq), jnp.int32),
        pltpu.VMEM((1, nf), f32),
        pltpu.VMEM((1, nq), f32),
        dma((3,)),
        pltpu.VMEM((4 * nf, nq), bf16),
        pltpu.VMEM((nr, 4 * nf), bf16),
        pltpu.VMEM((nf + 16, nr), bf16),
        pltpu.VMEM((nr, nq), bf16),
        pltpu.VMEM((nr, TILE), f32),
        pltpu.VMEM((nr, TILE), f32),
        pltpu.VMEM((1, nq), f32),
        pltpu.VMEM((nf + 16, nq), f32),
        pltpu.VMEM((nq, nf), f32),
        pltpu.VMEM((nf, nq), f32),
        pltpu.VMEM((nq, 2 * nf), bf16),
        pltpu.VMEM((nr, 2 * nf), f32),
        pltpu.VMEM((2, own, nf), f32),
        pltpu.VMEM((own, nf), f32),
        pltpu.VMEM((1, nf), f32),
        pltpu.VMEM((n - 1, 1, nf), f32),
    ]
    scratch += [pltpu.VMEM((1, half), f32)] * 2
    scratch += [pltpu.VMEM((n - 1, 1, half), f32)] * 2
    scratch += [pltpu.VMEM(shape + (own, nf), f32) for group in shapes for shape in group]
    scratch += [pltpu.VMEM((h, l, own, nf), f32) for group in shapes for h, _, l in group]
    scratch += [dma((n - 1,))] * 4 + [dma((last,))] * 4 + [dma((n - 1,))] * 2 + [dma((2,))]
    vmem = pl.BlockSpec(memory_space=pltpu.VMEM)
    hbm = pl.BlockSpec(memory_space=pltpu.HBM)
    shapes_out = (
        jax.ShapeDtypeStruct((own, nf), f32),
        jax.ShapeDtypeStruct((nr, nf), f32),
        jax.ShapeDtypeStruct((1, nf), f32),
    )
    results = pl.pallas_call(
        functools.partial(kernel, n),
        out_shape=shapes_out,
        in_specs=[vmem, vmem, hbm, hbm, hbm],
        out_specs=(vmem, hbm, vmem),
        scratch_shapes=scratch,
        compiler_params=pltpu.CompilerParams(
            collective_id=0, has_side_effects=True, vmem_limit_bytes=62 * 2 ** 20
        ),
    )(queries, references, query_ids[None, :], spread[None, :], cotangent[None, :])
    query_grad, reference_grad, spread_grad = pl.pallas_call(
        hand_out,
        out_shape=shapes_out,
        in_specs=[pl.BlockSpec(memory_space=pl.ANY)] * 3,
        out_specs=(hbm, hbm, hbm),
        scratch_shapes=[dma((3,))],
        compiler_params=pltpu.CompilerParams(vmem_limit_bytes=62 * 2 ** 20),
    )(*results)
    return query_grad, reference_grad, spread_grad[0]


def solution(mesh):
    placed = (P("parts", None), P(("parts", "ref"), None), P("parts"), P(), P("parts"))
    return jax.shard_map(
        functools.partial(on_device, mesh.shape["ref"]),
        mesh=mesh,
        in_specs=placed,
        out_specs=(P(("parts", "ref"), None), P(("parts", "ref"), None), P("parts")),
        check_vma=False,
    )
```

```python
import functools
import math

import jax
import jax.numpy as jnp
from jax import lax
from jax.experimental import pallas as pl
from jax.experimental.pallas import tpu as pltpu
from jax.sharding import PartitionSpec as P

LOG2E = math.log2(math.e)
TILE = 256
CHUNK = 512
SPAN = 1024


def split3(x):
    a = x.astype(jnp.bfloat16).astype(jnp.float32)
    b = (x - a).astype(jnp.bfloat16).astype(jnp.float32)
    c = (x - a - b).astype(jnp.bfloat16).astype(jnp.float32)
    return a, b, c


def plan(n):
    last = n.bit_length() - 2
    mid = (last + 1) // 2
    first = list(range(last))
    second = [0] + [b for b in range(mid, last)] + [b for b in range(1, mid)]
    return last, (first, second)


def layouts(n):
    last, orders = plan(n)
    shapes = []
    for order in orders:
        left = list(range(last))
        group = []
        for b in order:
            place = left.index(b)
            group.append((2 ** (len(left) - 1 - place), 2, 2 ** place))
            left.remove(b)
        shapes.append(group)
    return shapes


def kernel(
    n, q_ref, r_ref, ids_hbm, sp_hbm, cot_hbm, qg_ref, rg_hbm, sg_ref,
    rg_ref, rg_sem, ids_ref, sp_ref, cot_ref, in_sem,
    qat, ra, rta, pt, s0, s1, m_ref, ut, qt, xt, push, fin, fin_got, term, term_rx, *rest
):
    last, orders = plan(n)
    shapes = layouts(n)
    rest = list(rest)
    lse = [rest.pop(0) for _ in range(2)]
    lse_rx = [rest.pop(0) for _ in range(2)]
    acc = [[rest.pop(0) for _ in range(last)] for _ in range(2)]
    got = [[rest.pop(0) for _ in range(last)] for _ in range(2)]
    ls_send, ls_recv = rest[0:2], rest[2:4]
    rs_send, rs_recv = rest[4:6], rest[6:8]
    tm_send, tm_recv, fin_sem = rest[8:]
    nq, nf = q_ref.shape
    nr = r_ref.shape[0]
    own = nq // n
    half = nq // 2
    f32, bf16 = jnp.float32, jnp.bfloat16
    me = lax.axis_index("ref")

    loads = [
        pltpu.make_async_copy(src, dst, in_sem.at[i])
        for i, (src, dst) in enumerate(((ids_hbm, ids_ref), (sp_hbm, sp_ref), (cot_hbm, cot_ref)))
    ]
    for load in loads:
        load.start()

    def peer_of(k):
        return lax.rem(me + k, n)

    barrier = pltpu.get_barrier_semaphore()

    def greet(k, carry):
        pl.semaphore_signal(
            barrier, inc=1, device_id={"ref": peer_of(k)}, device_id_type=pl.DeviceIdType.MESH
        )
        return carry

    lax.fori_loop(1, n, greet, 0)
    for load in loads:
        load.wait()

    sp = sp_ref[...]
    inv = 1.0 / (sp * sp)
    inv_col = jnp.transpose(jnp.broadcast_to(inv, (8, nf)))[:, :1]
    for a in range(0, nq, TILE):
        rows = slice(a, a + TILE)
        q_t = jnp.transpose(q_ref[rows, :])
        qt[:, rows] = q_t
        scaled = q_t * (inv_col * LOG2E)
        high = scaled.astype(bf16)
        low = (scaled - high.astype(f32)).astype(bf16)
        qat[0:nf, rows] = high
        qat[nf:2 * nf, rows] = low
        qat[2 * nf:3 * nf, rows] = high
        norm = -0.5 * jnp.sum(q_t * scaled, axis=0, keepdims=True)
        n1, n2, n3 = split3(norm)
        place = lax.broadcasted_iota(jnp.int32, (nf, TILE), 0)
        ext = jnp.where(place < 6, 1.0, 0.0)
        ext = jnp.where(place == 0, n1, ext)
        ext = jnp.where(place == 1, n2, ext)
        ext = jnp.where(place == 2, n3, ext)
        qat[3 * nf:4 * nf, rows] = ext.astype(bf16)
    for a in range(0, nr, TILE):
        rows = slice(a, a + TILE)
        r = r_ref[rows, :]
        high = r.astype(bf16)
        low = (r - high.astype(f32)).astype(bf16)
        ra[rows, 0:nf] = high
        ra[rows, nf:2 * nf] = high
        ra[rows, 2 * nf:3 * nf] = low
        norm = -0.5 * LOG2E * jnp.sum(r * r * inv, axis=1, keepdims=True)
        n1, n2, n3 = split3(norm)
        place = lax.broadcasted_iota(jnp.int32, (TILE, nf), 1)
        ext = jnp.where(place < 6, 1.0, 0.0)
        ext = jnp.where(place == 3, n1, ext)
        ext = jnp.where(place == 4, n2, ext)
        ext = jnp.where(place == 5, n3, ext)
        ra[rows, 3 * nf:4 * nf] = ext.astype(bf16)
        rta[0:nf, rows] = jnp.transpose(high)
    rta[nf:nf + 16, :] = jnp.ones((16, nr), bf16)

    start = me * nr

    def at(t):
        return pl.ds(pl.multiple_of(t * TILE, TILE), TILE)

    def score(t, s_ref, a, best):
        s = jnp.dot(ra[a:a + SPAN, :], qat[:, at(t)], preferred_element_type=f32)
        local = ids_ref[:, at(t)] - (start + a)
        hit = lax.broadcasted_iota(jnp.int32, (SPAN, TILE), 0) == local
        s = jnp.where(hit, -jnp.inf, s)
        s_ref[a:a + SPAN, :] = s
        top = jnp.max(s, axis=0, keepdims=True)
        return top if best is None else jnp.maximum(best, top)

    def weigh(t, s_ref, a, peak, total):
        p = jnp.exp2(s_ref[a:a + SPAN, :] - peak).astype(bf16)
        pt[a:a + SPAN, at(t)] = p
        part = jnp.dot(rta[:, a:a + SPAN], p, preferred_element_type=f32)
        return part if total is None else total + part

    def stage(ahead, s_ahead, t, s_now):
        best, total = None, None
        peak = None if t is None else m_ref[:, at(t)]
        for a in range(0, nr, SPAN):
            if ahead is not None:
                best = score(ahead, s_ahead, a, best)
            if t is not None:
                total = weigh(t, s_now, a, peak, total)
        if ahead is not None:
            m_ref[:, at(ahead)] = best
        if t is not None:
            ut[:, at(t)] = total

    def all_to(src, dst, send, recv):
        def copy(k):
            return pltpu.make_async_remote_copy(
                src_ref=src, dst_ref=dst.at[k - 1], send_sem=send.at[k - 1], recv_sem=recv.at[k - 1],
                device_id={"ref": peer_of(k)}, device_id_type=pl.DeviceIdType.MESH,
            )

        def begin(k, carry):
            copy(k).start()
            return carry

        def end(k, carry):
            copy(k).wait()
            return carry

        return (lambda: lax.fori_loop(1, n, begin, 0)), (lambda: lax.fori_loop(1, n, end, 0))

    def spread_lse(g):
        cols = slice(g * half, (g + 1) * half)
        lse[g][...] = m_ref[:, cols] + jnp.log(ut[nf:nf + 1, cols]) * LOG2E
        all_to(lse[g], lse_rx[g], ls_send[g], ls_recv[g])[0]()

    def coefficients(g):
        cols = slice(g * half, (g + 1) * half)
        all_to(lse[g], lse_rx[g], ls_send[g], ls_recv[g])[1]()
        every = lse_rx[g][...]
        mine = lse[g][...]
        top = jnp.maximum(mine, jnp.max(every, axis=0))
        whole = jnp.exp2(mine - top) + jnp.sum(jnp.exp2(every - top[None]), axis=0)
        return cot_ref[:, cols] * jnp.exp2(m_ref[:, cols] - top) / whole

    def halving(g, i):
        size = 2 ** orders[g][i]
        bit = lax.rem(me // size, 2)
        return bit, pltpu.make_async_remote_copy(
            src_ref=acc[g][i].at[:, 1 - bit], dst_ref=got[g][i],
            send_sem=rs_send[g].at[i], recv_sem=rs_recv[g].at[i],
            device_id={"ref": me + (1 - 2 * bit) * size}, device_id_type=pl.DeviceIdType.MESH,
        )

    top_bit = lax.rem(me // (n // 2), 2)
    final = pltpu.make_async_remote_copy(
        src_ref=fin.at[1 - top_bit], dst_ref=fin_got, send_sem=fin_sem.at[0], recv_sem=fin_sem.at[1],
        device_id={"ref": me + (1 - 2 * top_bit) * (n // 2)}, device_id_type=pl.DeviceIdType.MESH,
    )

    def place_block(ref, shape, k, value):
        low = shape[2]
        ref[k // (2 * low), (k // low) % 2, k % low] = value

    def pull(g, coef):
        terms = jnp.zeros((1, nf), f32)
        for a in range(0, half, TILE):
            rows = slice(g * half + a, g * half + a + TILE)
            part = jnp.transpose(
                ut[0:nf, rows] * coef[:, a:a + TILE] - qt[:, rows] * (cot_ref[:, rows] * (1.0 / n))
            )
            terms = terms + jnp.sum(part * q_ref[rows, :], axis=0, keepdims=True)
            for b in range(0, TILE, own):
                place_block(acc[g][0], shapes[g][0], (a + b) // own, part[b:b + own])
        halving(g, 0)[1].start()
        return terms

    def settle(g, i):
        bit, copy = halving(g, i)
        copy.wait()
        high, _, low = shapes[g][i]
        for k in range(high * low):
            value = acc[g][i][k // low, bit, k % low] + got[g][i][k // low, k % low]
            if i + 1 < last:
                place_block(acc[g][i + 1], shapes[g][i + 1], k, value)
            else:
                fin[g] = value
        if i + 1 < last:
            halving(g, i + 1)[1].start()
        else:
            @pl.when(top_bit != g)
            def _():
                final.start()

    row = lax.broadcasted_iota(jnp.int32, (16, half), 0)

    def scale_queries(g, coef):
        cols = slice(g * half, (g + 1) * half)
        c1, c2, _ = split3(coef)
        xt[0:nf, cols] = (qt[:, cols] * coef).astype(bf16)
        xt[nf:nf + 16, cols] = jnp.where(row == 0, c1, jnp.where(row == 1, c2, 0.0)).astype(bf16)

    def pushed(g, i):
        rows = slice(i * CHUNK, (i + 1) * CHUNK)
        cols = slice(g * half, (g + 1) * half)
        return lax.dot_general(
            pt[rows, cols], xt[:, cols], (((1,), (1,)), ((), ())), preferred_element_type=f32
        )

    stores = [
        pltpu.make_async_copy(
            rg_ref.at[pl.ds(i * CHUNK, CHUNK)], rg_hbm.at[pl.ds(i * CHUNK, CHUNK)], rg_sem.at[i]
        )
        for i in range(nr // CHUNK)
    ]

    def finish(i, terms):
        rows = slice(i * CHUNK, (i + 1) * CHUNK)
        both = push[rows, :] + pushed(1, i)
        r = r_ref[rows, :]
        column = both[:, nf:nf + 1] + both[:, nf + 1:nf + 2]
        grad = (both[:, 0:nf] - r * column) * inv
        rg_ref[rows, :] = grad
        stores[i].start()
        return terms + jnp.sum(r * grad, axis=0, keepdims=True)

    tiles = nq // TILE
    chunks = nr // CHUNK
    stage(0, s0, None, None)

    def pair(t, carry):
        stage(2 * t + 1, s1, 2 * t, s0)
        stage(2 * t + 2, s0, 2 * t + 1, s1)
        return carry

    lax.fori_loop(0, tiles // 4, pair, 0)
    pl.semaphore_wait(barrier, n - 1)
    spread_lse(0)
    lax.fori_loop(tiles // 4, tiles // 2 - 1, pair, 0)
    coef = coefficients(0)
    terms = pull(0, coef)
    stage(tiles - 1, s1, tiles - 2, s0)
    settle(0, 0)
    stage(None, None, tiles - 1, s1)
    spread_lse(1)

    scale_queries(0, coef)
    for i in range(chunks):
        push[i * CHUNK:(i + 1) * CHUNK, :] = pushed(0, i)
    settle(0, 1)
    coef = coefficients(1)
    terms = (terms + pull(1, coef)) * inv
    scale_queries(1, coef)
    terms = finish(0, terms)
    settle(1, 0)
    for i in range(1, chunks):
        terms = finish(i, terms)
    term[...] = terms
    term_start, term_wait = all_to(term, term_rx, tm_send, tm_recv)
    term_start()
    for i in range(2, last):
        settle(0, i)
    for i in range(1, last):
        settle(1, i)
    for store in stores:
        store.wait()
    term_wait()
    summed = terms + jnp.sum(term_rx[...], axis=0)
    sg_ref[...] = -summed / sp - jnp.sum(cot_ref[...], axis=1, keepdims=True) / sp
    final.wait()
    qg_ref[...] = (fin[top_bit] + fin_got[...]) * inv


def hand_out(qg_in, rg_in, sg_in, qg_out, rg_out, sg_out, qg, rg, sg, load_sem, store_sem):
    rows = rg.shape[0]
    parts = [(qg_in, qg, qg_out), (sg_in, sg, sg_out)]
    for a in range(0, rows, CHUNK):
        piece = pl.ds(a, CHUNK)
        parts.append((rg_in.at[piece], rg.at[piece], rg_out.at[piece]))
    loads = [pltpu.make_async_copy(x, y, load_sem.at[i]) for i, (x, y, _) in enumerate(parts)]
    stores = [pltpu.make_async_copy(y, z, store_sem.at[i]) for i, (_, y, z) in enumerate(parts)]
    for load in loads:
        load.start()
    for load, store in zip(loads, stores):
        load.wait()
        store.start()
    for store in stores:
        store.wait()


def on_device(n, queries, references, query_ids, spread, cotangent):
    nq, nf = queries.shape
    nr = references.shape[0]
    own = nq // n
    half = nq // 2
    f32, bf16 = jnp.float32, jnp.bfloat16
    last, _ = plan(n)
    shapes = layouts(n)
    dma = pltpu.SemaphoreType.DMA
    scratch = [
        pltpu.VMEM((nr, nf), f32),
        dma((nr // CHUNK,)),
        pltpu.VMEM((1, nq), jnp.int32),
        pltpu.VMEM((1, nf), f32),
        pltpu.VMEM((1, nq), f32),
        dma((3,)),
        pltpu.VMEM((4 * nf, nq), bf16),
        pltpu.VMEM((nr, 4 * nf), bf16),
        pltpu.VMEM((nf + 16, nr), bf16),
        pltpu.VMEM((nr, nq), bf16),
        pltpu.VMEM((nr, TILE), f32),
        pltpu.VMEM((nr, TILE), f32),
        pltpu.VMEM((1, nq), f32),
        pltpu.VMEM((nf + 16, nq), f32),
        pltpu.VMEM((nf, nq), f32),
        pltpu.VMEM((nf + 16, nq), bf16),
        pltpu.VMEM((nr, nf + 16), f32),
        pltpu.VMEM((2, own, nf), f32),
        pltpu.VMEM((own, nf), f32),
        pltpu.VMEM((1, nf), f32),
        pltpu.VMEM((n - 1, 1, nf), f32),
    ]
    scratch += [pltpu.VMEM((1, half), f32)] * 2
    scratch += [pltpu.VMEM((n - 1, 1, half), f32)] * 2
    scratch += [pltpu.VMEM(shape + (own, nf), f32) for group in shapes for shape in group]
    scratch += [pltpu.VMEM((h, l, own, nf), f32) for group in shapes for h, _, l in group]
    scratch += [dma((n - 1,))] * 4 + [dma((last,))] * 4 + [dma((n - 1,))] * 2 + [dma((2,))]
    vmem = pl.BlockSpec(memory_space=pltpu.VMEM)
    hbm = pl.BlockSpec(memory_space=pltpu.HBM)
    shapes_out = (
        jax.ShapeDtypeStruct((own, nf), f32),
        jax.ShapeDtypeStruct((nr, nf), f32),
        jax.ShapeDtypeStruct((1, nf), f32),
    )
    results = pl.pallas_call(
        functools.partial(kernel, n),
        out_shape=shapes_out,
        in_specs=[vmem, vmem, hbm, hbm, hbm],
        out_specs=(vmem, hbm, vmem),
        scratch_shapes=scratch,
        compiler_params=pltpu.CompilerParams(
            collective_id=0, has_side_effects=True, vmem_limit_bytes=62 * 2 ** 20
        ),
    )(queries, references, query_ids[None, :], spread[None, :], cotangent[None, :])
    query_grad, reference_grad, spread_grad = pl.pallas_call(
        hand_out,
        out_shape=shapes_out,
        in_specs=[pl.BlockSpec(memory_space=pl.ANY)] * 3,
        out_specs=(hbm, hbm, hbm),
        scratch_shapes=[pltpu.VMEM(x.shape, f32) for x in shapes_out]
        + [dma((2 + nr // CHUNK,))] * 2,
        compiler_params=pltpu.CompilerParams(vmem_limit_bytes=62 * 2 ** 20),
    )(*results)
    return query_grad, reference_grad, spread_grad[0]


def solution(mesh):
    placed = (P("parts", None), P(("parts", "ref"), None), P("parts"), P(), P("parts"))
    return jax.shard_map(
        functools.partial(on_device, mesh.shape["ref"]),
        mesh=mesh,
        in_specs=placed,
        out_specs=(P(("parts", "ref"), None), P(("parts", "ref"), None), P("parts")),
        check_vma=False,
    )
```

```python
import functools
import math

import jax
import jax.numpy as jnp
from jax import lax
from jax.experimental import pallas as pl
from jax.experimental.pallas import tpu as pltpu
from jax.sharding import PartitionSpec as P

LOG2E = math.log2(math.e)
TILE = 256
CHUNK = 512
SPAN = 1024


def split3(x):
    a = x.astype(jnp.bfloat16).astype(jnp.float32)
    b = (x - a).astype(jnp.bfloat16).astype(jnp.float32)
    c = (x - a - b).astype(jnp.bfloat16).astype(jnp.float32)
    return a, b, c


GROUPS = 4
TURN = (0, 3, 1, 2)


def plan(n):
    last = n.bit_length() - 3
    return last, [list(range(last))] * GROUPS


def layouts(n):
    last, orders = plan(n)
    shapes = []
    for order in orders:
        left = list(range(last))
        group = []
        for b in order:
            place = left.index(b)
            group.append((2 ** (len(left) - 1 - place), 2, 2 ** place))
            left.remove(b)
        shapes.append(group)
    return shapes


def kernel(
    n, q_ref, r_ref, ids_hbm, sp_hbm, cot_hbm, qg_ref, rg_hbm, sg_ref,
    rg_ref, rg_sem, ids_ref, sp_ref, cot_ref, in_sem,
    qat, ra, rta, pt, s0, s1, m_ref, ut, qt, xt, push, fin, fin_got, term, term_rx, *rest
):
    last, orders = plan(n)
    shapes = layouts(n)
    rest = list(rest)
    lse = [rest.pop(0) for _ in range(GROUPS)]
    lse_rx = [rest.pop(0) for _ in range(GROUPS)]
    acc = [[rest.pop(0) for _ in range(last)] for _ in range(GROUPS)]
    got = [[rest.pop(0) for _ in range(last)] for _ in range(GROUPS)]
    ls_send, ls_recv, rs_send, rs_recv = (rest[i * GROUPS:(i + 1) * GROUPS] for i in range(4))
    tm_send, tm_recv, fin_send, fin_recv = rest[4 * GROUPS:]
    nq, nf = q_ref.shape
    nr = r_ref.shape[0]
    own = nq // n
    half = nq // GROUPS
    f32, bf16 = jnp.float32, jnp.bfloat16
    me = lax.axis_index("ref")

    loads = [
        pltpu.make_async_copy(src, dst, in_sem.at[i])
        for i, (src, dst) in enumerate(((ids_hbm, ids_ref), (sp_hbm, sp_ref), (cot_hbm, cot_ref)))
    ]
    for load in loads:
        load.start()

    def peer_of(k):
        return lax.rem(me + k, n)

    barrier = pltpu.get_barrier_semaphore()

    def greet(k, carry):
        pl.semaphore_signal(
            barrier, inc=1, device_id={"ref": peer_of(k)}, device_id_type=pl.DeviceIdType.MESH
        )
        return carry

    lax.fori_loop(1, n, greet, 0)
    for load in loads:
        load.wait()

    sp = sp_ref[...]
    inv = 1.0 / (sp * sp)
    inv_col = jnp.transpose(jnp.broadcast_to(inv, (8, nf)))[:, :1]
    for a in range(0, nq, TILE):
        rows = slice(a, a + TILE)
        q_t = jnp.transpose(q_ref[rows, :])
        qt[:, rows] = q_t
        scaled = q_t * (inv_col * LOG2E)
        high = scaled.astype(bf16)
        low = (scaled - high.astype(f32)).astype(bf16)
        qat[0:nf, rows] = high
        qat[nf:2 * nf, rows] = low
        qat[2 * nf:3 * nf, rows] = high
        norm = -0.5 * jnp.sum(q_t * scaled, axis=0, keepdims=True)
        n1, n2, n3 = split3(norm)
        place = lax.broadcasted_iota(jnp.int32, (nf, TILE), 0)
        ext = jnp.where(place < 6, 1.0, 0.0)
        ext = jnp.where(place == 0, n1, ext)
        ext = jnp.where(place == 1, n2, ext)
        ext = jnp.where(place == 2, n3, ext)
        qat[3 * nf:4 * nf, rows] = ext.astype(bf16)
    for a in range(0, nr, TILE):
        rows = slice(a, a + TILE)
        r = r_ref[rows, :]
        high = r.astype(bf16)
        low = (r - high.astype(f32)).astype(bf16)
        ra[rows, 0:nf] = high
        ra[rows, nf:2 * nf] = high
        ra[rows, 2 * nf:3 * nf] = low
        norm = -0.5 * LOG2E * jnp.sum(r * r * inv, axis=1, keepdims=True)
        n1, n2, n3 = split3(norm)
        place = lax.broadcasted_iota(jnp.int32, (TILE, nf), 1)
        ext = jnp.where(place < 6, 1.0, 0.0)
        ext = jnp.where(place == 3, n1, ext)
        ext = jnp.where(place == 4, n2, ext)
        ext = jnp.where(place == 5, n3, ext)
        ra[rows, 3 * nf:4 * nf] = ext.astype(bf16)
        rta[0:nf, rows] = jnp.transpose(high)
    rta[nf:nf + 16, :] = jnp.ones((16, nr), bf16)

    start = me * nr

    def at(t):
        return pl.ds(pl.multiple_of(t * TILE, TILE), TILE)

    def score(t, s_ref, a, best):
        s = jnp.dot(ra[a:a + SPAN, :], qat[:, at(t)], preferred_element_type=f32)
        local = ids_ref[:, at(t)] - (start + a)
        hit = lax.broadcasted_iota(jnp.int32, (SPAN, TILE), 0) == local
        s = jnp.where(hit, -jnp.inf, s)
        s_ref[a:a + SPAN, :] = s
        top = jnp.max(s, axis=0, keepdims=True)
        return top if best is None else jnp.maximum(best, top)

    def weigh(t, s_ref, a, peak, total):
        p = jnp.exp2(s_ref[a:a + SPAN, :] - peak).astype(bf16)
        pt[a:a + SPAN, at(t)] = p
        part = jnp.dot(rta[:, a:a + SPAN], p, preferred_element_type=f32)
        return part if total is None else total + part

    def stage(ahead, s_ahead, t, s_now):
        best, total = None, None
        peak = None if t is None else m_ref[:, at(t)]
        for a in range(0, nr, SPAN):
            if ahead is not None:
                best = score(ahead, s_ahead, a, best)
            if t is not None:
                total = weigh(t, s_now, a, peak, total)
        if ahead is not None:
            m_ref[:, at(ahead)] = best
        if t is not None:
            ut[:, at(t)] = total

    def all_to(src, dst, send, recv):
        def copy(k):
            return pltpu.make_async_remote_copy(
                src_ref=src, dst_ref=dst.at[k - 1], send_sem=send.at[k - 1], recv_sem=recv.at[k - 1],
                device_id={"ref": peer_of(k)}, device_id_type=pl.DeviceIdType.MESH,
            )

        def begin(k, carry):
            copy(k).start()
            return carry

        def end(k, carry):
            copy(k).wait()
            return carry

        return (lambda: lax.fori_loop(1, n, begin, 0)), (lambda: lax.fori_loop(1, n, end, 0))

    def spread_lse(g):
        cols = slice(g * half, (g + 1) * half)
        lse[g][...] = m_ref[:, cols] + jnp.log(ut[nf:nf + 1, cols]) * LOG2E
        all_to(lse[g], lse_rx[g], ls_send[g], ls_recv[g])[0]()

    def coefficients(g):
        cols = slice(g * half, (g + 1) * half)
        all_to(lse[g], lse_rx[g], ls_send[g], ls_recv[g])[1]()
        every = lse_rx[g][...]
        mine = lse[g][...]
        top = jnp.maximum(mine, jnp.max(every, axis=0))
        whole = jnp.exp2(mine - top) + jnp.sum(jnp.exp2(every - top[None]), axis=0)
        return cot_ref[:, cols] * jnp.exp2(m_ref[:, cols] - top) / whole

    def halving(g, i):
        size = 2 ** orders[g][i]
        bit = lax.rem(me // size, 2)
        return bit, pltpu.make_async_remote_copy(
            src_ref=acc[g][i].at[:, 1 - bit], dst_ref=got[g][i],
            send_sem=rs_send[g].at[i], recv_sem=rs_recv[g].at[i],
            device_id={"ref": me + (1 - 2 * bit) * size}, device_id_type=pl.DeviceIdType.MESH,
        )

    far = n // GROUPS
    group = lax.rem(me // far, GROUPS)

    def final(j):
        to = lax.rem(group + j, GROUPS)
        return pltpu.make_async_remote_copy(
            src_ref=fin.at[to], dst_ref=fin_got.at[j - 1],
            send_sem=fin_send.at[j - 1], recv_sem=fin_recv.at[j - 1],
            device_id={"ref": me + (to - group) * far}, device_id_type=pl.DeviceIdType.MESH,
        )

    def place_block(ref, shape, k, value):
        low = shape[2]
        ref[k // (2 * low), (k // low) % 2, k % low] = value

    def pull(g, coef):
        terms = jnp.zeros((1, nf), f32)
        for a in range(0, half, TILE):
            rows = slice(g * half + a, g * half + a + TILE)
            part = jnp.transpose(
                ut[0:nf, rows] * coef[:, a:a + TILE] - qt[:, rows] * (cot_ref[:, rows] * (1.0 / n))
            )
            terms = terms + jnp.sum(part * q_ref[rows, :], axis=0, keepdims=True)
            for b in range(0, TILE, own):
                place_block(acc[g][0], shapes[g][0], (a + b) // own, part[b:b + own])
        halving(g, 0)[1].start()
        return terms

    def settle(g, i):
        bit, copy = halving(g, i)
        copy.wait()
        high, _, low = shapes[g][i]
        for k in range(high * low):
            value = acc[g][i][k // low, bit, k % low] + got[g][i][k // low, k % low]
            if i + 1 < last:
                place_block(acc[g][i + 1], shapes[g][i + 1], k, value)
            else:
                fin[g] = value
        if i + 1 < last:
            halving(g, i + 1)[1].start()
        else:
            for j in range(1, GROUPS):
                pl.when(group == (g - j) % GROUPS)(final(j).start)

    row = lax.broadcasted_iota(jnp.int32, (16, half), 0)

    def scale_queries(g, coef):
        cols = slice(g * half, (g + 1) * half)
        c1, c2, _ = split3(coef)
        xt[0:nf, cols] = (qt[:, cols] * coef).astype(bf16)
        xt[nf:nf + 16, cols] = jnp.where(row == 0, c1, jnp.where(row == 1, c2, 0.0)).astype(bf16)

    def pushed(g, end, i):
        rows = slice(i * CHUNK, (i + 1) * CHUNK)
        cols = slice(g * half, end * half)
        return lax.dot_general(
            pt[rows, cols], xt[:, cols], (((1,), (1,)), ((), ())), preferred_element_type=f32
        )

    stores = [
        pltpu.make_async_copy(
            rg_ref.at[pl.ds(i * CHUNK, CHUNK)], rg_hbm.at[pl.ds(i * CHUNK, CHUNK)], rg_sem.at[i]
        )
        for i in range(nr // CHUNK)
    ]

    def finish(i, terms):
        rows = slice(i * CHUNK, (i + 1) * CHUNK)
        both = push[rows, :] + pushed(TURN[3], TURN[3] + 1, i)
        r = r_ref[rows, :]
        column = both[:, nf:nf + 1] + both[:, nf + 1:nf + 2]
        grad = (both[:, 0:nf] - r * column) * inv
        rg_ref[rows, :] = grad
        stores[i].start()
        return terms + jnp.sum(r * grad, axis=0, keepdims=True)

    per = half // TILE
    order = [g * per + i for g in TURN for i in range(per)]
    chunks = nr // CHUNK
    coefs = {}
    terms = jnp.zeros((1, nf), f32)

    def collect(g):
        coefs[g] = coefficients(g)
        return pull(g, coefs[g])

    bufs = (s0, s1)
    stage(order[0], s0, None, None)
    for i, t in enumerate(order):
        ahead = order[i + 1] if i + 1 < len(order) else None
        stage(ahead, bufs[(i + 1) % 2], t, bufs[i % 2])
        if (i + 1) % per:
            continue
        turn = (i + 1) // per - 1
        if turn == 0:
            pl.semaphore_wait(barrier, n - 1)
        spread_lse(TURN[turn])
        if turn >= 2:
            settle(TURN[turn - 2], 0)
        if turn >= 1:
            terms = terms + collect(TURN[turn - 1])
        if turn >= 2:
            for k in range(1, last):
                settle(TURN[turn - 2], k)

    early = TURN[:3]
    for g in early:
        scale_queries(g, coefs[g])
    for i in range(chunks):
        rows = slice(i * CHUNK, (i + 1) * CHUNK)
        push[rows, :] = pushed(0, 2, i) + pushed(3, 4, i)
        if i == 0:
            settle(early[2], 0)
    terms = (terms + collect(TURN[3])) * inv
    scale_queries(TURN[3], coefs[TURN[3]])
    for k in range(1, last):
        settle(early[2], k)
    for i in range(chunks):
        terms = finish(i, terms)
        if i == chunks // 2 - 1:
            settle(TURN[3], 0)
    term[...] = terms
    term_start, term_wait = all_to(term, term_rx, tm_send, tm_recv)
    term_start()
    for k in range(1, last):
        settle(TURN[3], k)
    for store in stores:
        store.wait()
    term_wait()
    summed = terms + jnp.sum(term_rx[...], axis=0)
    sg_ref[...] = -summed / sp - jnp.sum(cot_ref[...], axis=1, keepdims=True) / sp
    for j in range(1, GROUPS):
        final(j).wait()
    qg_ref[...] = (fin[group] + jnp.sum(fin_got[...], axis=0)) * inv


def hand_out(qg_in, rg_in, sg_in, qg_out, rg_out, sg_out, qg, rg, sg, load_sem, store_sem):
    rows = rg.shape[0]
    parts = [(qg_in, qg, qg_out), (sg_in, sg, sg_out)]
    for a in range(0, rows, CHUNK):
        piece = pl.ds(a, CHUNK)
        parts.append((rg_in.at[piece], rg.at[piece], rg_out.at[piece]))
    loads = [pltpu.make_async_copy(x, y, load_sem.at[i]) for i, (x, y, _) in enumerate(parts)]
    stores = [pltpu.make_async_copy(y, z, store_sem.at[i]) for i, (_, y, z) in enumerate(parts)]
    for load in loads:
        load.start()
    for load, store in zip(loads, stores):
        load.wait()
        store.start()
    for store in stores:
        store.wait()


def on_device(n, queries, references, query_ids, spread, cotangent):
    nq, nf = queries.shape
    nr = references.shape[0]
    own = nq // n
    half = nq // GROUPS
    f32, bf16 = jnp.float32, jnp.bfloat16
    last, _ = plan(n)
    shapes = layouts(n)
    dma = pltpu.SemaphoreType.DMA
    scratch = [
        pltpu.VMEM((nr, nf), f32),
        dma((nr // CHUNK,)),
        pltpu.VMEM((1, nq), jnp.int32),
        pltpu.VMEM((1, nf), f32),
        pltpu.VMEM((1, nq), f32),
        dma((3,)),
        pltpu.VMEM((4 * nf, nq), bf16),
        pltpu.VMEM((nr, 4 * nf), bf16),
        pltpu.VMEM((nf + 16, nr), bf16),
        pltpu.VMEM((nr, nq), bf16),
        pltpu.VMEM((nr, TILE), f32),
        pltpu.VMEM((nr, TILE), f32),
        pltpu.VMEM((1, nq), f32),
        pltpu.VMEM((nf + 16, nq), f32),
        pltpu.VMEM((nf, nq), f32),
        pltpu.VMEM((nf + 16, nq), bf16),
        pltpu.VMEM((nr, nf + 16), f32),
        pltpu.VMEM((GROUPS, own, nf), f32),
        pltpu.VMEM((GROUPS - 1, own, nf), f32),
        pltpu.VMEM((1, nf), f32),
        pltpu.VMEM((n - 1, 1, nf), f32),
    ]
    scratch += [pltpu.VMEM((1, half), f32)] * GROUPS
    scratch += [pltpu.VMEM((n - 1, 1, half), f32)] * GROUPS
    scratch += [pltpu.VMEM(shape + (own, nf), f32) for group in shapes for shape in group]
    scratch += [pltpu.VMEM((h, l, own, nf), f32) for group in shapes for h, _, l in group]
    scratch += [dma((n - 1,))] * (2 * GROUPS) + [dma((last,))] * (2 * GROUPS)
    scratch += [dma((n - 1,))] * 2 + [dma((GROUPS - 1,))] * 2
    vmem = pl.BlockSpec(memory_space=pltpu.VMEM)
    hbm = pl.BlockSpec(memory_space=pltpu.HBM)
    shapes_out = (
        jax.ShapeDtypeStruct((own, nf), f32),
        jax.ShapeDtypeStruct((nr, nf), f32),
        jax.ShapeDtypeStruct((1, nf), f32),
    )
    results = pl.pallas_call(
        functools.partial(kernel, n),
        out_shape=shapes_out,
        in_specs=[vmem, vmem, hbm, hbm, hbm],
        out_specs=(vmem, hbm, vmem),
        scratch_shapes=scratch,
        compiler_params=pltpu.CompilerParams(
            collective_id=0, has_side_effects=True, vmem_limit_bytes=62 * 2 ** 20
        ),
    )(queries, references, query_ids[None, :], spread[None, :], cotangent[None, :])
    query_grad, reference_grad, spread_grad = pl.pallas_call(
        hand_out,
        out_shape=shapes_out,
        in_specs=[pl.BlockSpec(memory_space=pl.ANY)] * 3,
        out_specs=(hbm, hbm, hbm),
        scratch_shapes=[pltpu.VMEM(x.shape, f32) for x in shapes_out]
        + [dma((2 + nr // CHUNK,))] * 2,
        compiler_params=pltpu.CompilerParams(vmem_limit_bytes=62 * 2 ** 20),
    )(*results)
    return query_grad, reference_grad, spread_grad[0]


def solution(mesh):
    placed = (P("parts", None), P(("parts", "ref"), None), P("parts"), P(), P("parts"))
    return jax.shard_map(
        functools.partial(on_device, mesh.shape["ref"]),
        mesh=mesh,
        in_specs=placed,
        out_specs=(P(("parts", "ref"), None), P(("parts", "ref"), None), P("parts")),
        check_vma=False,
    )
```

```python
import functools
import math

import jax
import jax.numpy as jnp
from jax import lax
from jax.experimental import pallas as pl
from jax.experimental.pallas import tpu as pltpu
from jax.sharding import PartitionSpec as P

LOG2E = math.log2(math.e)
TILE = 512
CHUNK = 512
SPAN = 1024


def split3(x):
    a = x.astype(jnp.bfloat16).astype(jnp.float32)
    b = (x - a).astype(jnp.bfloat16).astype(jnp.float32)
    c = (x - a - b).astype(jnp.bfloat16).astype(jnp.float32)
    return a, b, c


GROUPS = 4
TURN = (0, 3, 1, 2)


def plan(n):
    last = n.bit_length() - 3
    return last, [list(range(last))] * GROUPS


def layouts(n):
    last, orders = plan(n)
    shapes = []
    for order in orders:
        left = list(range(last))
        group = []
        for b in order:
            place = left.index(b)
            group.append((2 ** (len(left) - 1 - place), 2, 2 ** place))
            left.remove(b)
        shapes.append(group)
    return shapes


def kernel(
    n, q_ref, r_ref, ids_hbm, sp_hbm, cot_hbm, qg_ref, rg_hbm, sg_ref,
    rg_ref, rg_sem, ids_ref, sp_ref, cot_ref, in_sem,
    qat, ra, rta, pt, s0, s1, m_ref, ut, qt, xt, push, fin, fin_got, term, term_rx, *rest
):
    last, orders = plan(n)
    shapes = layouts(n)
    rest = list(rest)
    lse = [rest.pop(0) for _ in range(GROUPS)]
    lse_rx = [rest.pop(0) for _ in range(GROUPS)]
    acc = [[rest.pop(0) for _ in range(last)] for _ in range(GROUPS)]
    got = [[rest.pop(0) for _ in range(last)] for _ in range(GROUPS)]
    ls_send, ls_recv, rs_send, rs_recv = (rest[i * GROUPS:(i + 1) * GROUPS] for i in range(4))
    tm_send, tm_recv, fin_send, fin_recv = rest[4 * GROUPS:]
    nq, nf = q_ref.shape
    nr = r_ref.shape[0]
    own = nq // n
    half = nq // GROUPS
    f32, bf16 = jnp.float32, jnp.bfloat16
    me = lax.axis_index("ref")

    loads = [
        pltpu.make_async_copy(src, dst, in_sem.at[i])
        for i, (src, dst) in enumerate(((ids_hbm, ids_ref), (sp_hbm, sp_ref), (cot_hbm, cot_ref)))
    ]
    for load in loads:
        load.start()

    def peer_of(k):
        return lax.rem(me + k, n)

    barrier = pltpu.get_barrier_semaphore()

    def greet(k, carry):
        pl.semaphore_signal(
            barrier, inc=1, device_id={"ref": peer_of(k)}, device_id_type=pl.DeviceIdType.MESH
        )
        return carry

    lax.fori_loop(1, n, greet, 0)
    for load in loads:
        load.wait()

    sp = sp_ref[...]
    inv = 1.0 / (sp * sp)
    inv_col = jnp.transpose(jnp.broadcast_to(inv, (8, nf)))[:, :1]
    for a in range(0, nq, TILE):
        rows = slice(a, a + TILE)
        q_t = jnp.transpose(q_ref[rows, :])
        qt[:, rows] = q_t
        scaled = q_t * (inv_col * LOG2E)
        high = scaled.astype(bf16)
        low = (scaled - high.astype(f32)).astype(bf16)
        qat[0:nf, rows] = high
        qat[nf:2 * nf, rows] = low
        qat[2 * nf:3 * nf, rows] = high
        norm = -0.5 * jnp.sum(q_t * scaled, axis=0, keepdims=True)
        n1, n2, n3 = split3(norm)
        place = lax.broadcasted_iota(jnp.int32, (nf, TILE), 0)
        ext = jnp.where(place < 6, 1.0, 0.0)
        ext = jnp.where(place == 0, n1, ext)
        ext = jnp.where(place == 1, n2, ext)
        ext = jnp.where(place == 2, n3, ext)
        qat[3 * nf:4 * nf, rows] = ext.astype(bf16)
    for a in range(0, nr, TILE):
        rows = slice(a, a + TILE)
        r = r_ref[rows, :]
        high = r.astype(bf16)
        low = (r - high.astype(f32)).astype(bf16)
        ra[rows, 0:nf] = high
        ra[rows, nf:2 * nf] = high
        ra[rows, 2 * nf:3 * nf] = low
        norm = -0.5 * LOG2E * jnp.sum(r * r * inv, axis=1, keepdims=True)
        n1, n2, n3 = split3(norm)
        place = lax.broadcasted_iota(jnp.int32, (TILE, nf), 1)
        ext = jnp.where(place < 6, 1.0, 0.0)
        ext = jnp.where(place == 3, n1, ext)
        ext = jnp.where(place == 4, n2, ext)
        ext = jnp.where(place == 5, n3, ext)
        ra[rows, 3 * nf:4 * nf] = ext.astype(bf16)
        rta[0:nf, rows] = jnp.transpose(high)
    rta[nf:nf + 16, :] = jnp.ones((16, nr), bf16)

    start = me * nr

    def at(t):
        return pl.ds(pl.multiple_of(t * TILE, TILE), TILE)

    def score(t, s_ref, a, best):
        s = jnp.dot(ra[a:a + SPAN, :], qat[:, at(t)], preferred_element_type=f32)
        local = ids_ref[:, at(t)] - (start + a)
        hit = lax.broadcasted_iota(jnp.int32, (SPAN, TILE), 0) == local
        s = jnp.where(hit, -jnp.inf, s)
        s_ref[a:a + SPAN, :] = s
        top = jnp.max(s, axis=0, keepdims=True)
        return top if best is None else jnp.maximum(best, top)

    def weigh(t, s_ref, a, peak, total):
        p = jnp.exp2(s_ref[a:a + SPAN, :] - peak).astype(bf16)
        pt[a:a + SPAN, at(t)] = p
        part = jnp.dot(rta[:, a:a + SPAN], p, preferred_element_type=f32)
        return part if total is None else total + part

    def stage(ahead, s_ahead, t, s_now):
        best, total = None, None
        peak = None if t is None else m_ref[:, at(t)]
        for a in range(0, nr, SPAN):
            if ahead is not None:
                best = score(ahead, s_ahead, a, best)
            if t is not None:
                total = weigh(t, s_now, a, peak, total)
        if ahead is not None:
            m_ref[:, at(ahead)] = best
        if t is not None:
            ut[:, at(t)] = total

    def all_to(src, dst, send, recv):
        def copy(k):
            return pltpu.make_async_remote_copy(
                src_ref=src, dst_ref=dst.at[k - 1], send_sem=send.at[0], recv_sem=recv.at[0],
                device_id={"ref": peer_of(k)}, device_id_type=pl.DeviceIdType.MESH,
            )

        def begin(k, carry):
            copy(k).start()
            return carry

        def end():
            pltpu.make_async_copy(dst, dst, send.at[0]).wait()
            pltpu.make_async_copy(dst, dst, recv.at[0]).wait()

        return (lambda: lax.fori_loop(1, n, begin, 0)), end

    def spread_lse(g):
        cols = slice(g * half, (g + 1) * half)
        lse[g][...] = m_ref[:, cols] + jnp.log(ut[nf:nf + 1, cols]) * LOG2E
        all_to(lse[g], lse_rx[g], ls_send[g], ls_recv[g])[0]()

    def coefficients(g):
        cols = slice(g * half, (g + 1) * half)
        all_to(lse[g], lse_rx[g], ls_send[g], ls_recv[g])[1]()
        every = lse_rx[g][...]
        mine = lse[g][...]
        top = jnp.maximum(mine, jnp.max(every, axis=0))
        whole = jnp.exp2(mine - top) + jnp.sum(jnp.exp2(every - top[None]), axis=0)
        return cot_ref[:, cols] * jnp.exp2(m_ref[:, cols] - top) / whole

    def halving(g, i):
        size = 2 ** orders[g][i]
        bit = lax.rem(me // size, 2)
        return bit, pltpu.make_async_remote_copy(
            src_ref=acc[g][i].at[:, 1 - bit], dst_ref=got[g][i],
            send_sem=rs_send[g].at[i], recv_sem=rs_recv[g].at[i],
            device_id={"ref": me + (1 - 2 * bit) * size}, device_id_type=pl.DeviceIdType.MESH,
        )

    far = n // GROUPS
    group = lax.rem(me // far, GROUPS)

    def final(j):
        to = lax.rem(group + j, GROUPS)
        return pltpu.make_async_remote_copy(
            src_ref=fin.at[to], dst_ref=fin_got.at[j - 1],
            send_sem=fin_send.at[j - 1], recv_sem=fin_recv.at[j - 1],
            device_id={"ref": me + (to - group) * far}, device_id_type=pl.DeviceIdType.MESH,
        )

    def place_block(ref, shape, k, value):
        low = shape[2]
        ref[k // (2 * low), (k // low) % 2, k % low] = value

    def pull(g, coef):
        terms = jnp.zeros((1, nf), f32)
        for a in range(0, half, TILE):
            rows = slice(g * half + a, g * half + a + TILE)
            part = jnp.transpose(
                ut[0:nf, rows] * coef[:, a:a + TILE] - qt[:, rows] * (cot_ref[:, rows] * (1.0 / n))
            )
            terms = terms + jnp.sum(part * q_ref[rows, :], axis=0, keepdims=True)
            for b in range(0, TILE, own):
                place_block(acc[g][0], shapes[g][0], (a + b) // own, part[b:b + own])
        halving(g, 0)[1].start()
        return terms

    def settle(g, i):
        bit, copy = halving(g, i)
        copy.wait()
        high, _, low = shapes[g][i]
        for k in range(high * low):
            value = acc[g][i][k // low, bit, k % low] + got[g][i][k // low, k % low]
            if i + 1 < last:
                place_block(acc[g][i + 1], shapes[g][i + 1], k, value)
            else:
                fin[g] = value
        if i + 1 < last:
            halving(g, i + 1)[1].start()
        else:
            for j in range(1, GROUPS):
                pl.when(group == (g - j) % GROUPS)(final(j).start)

    row = lax.broadcasted_iota(jnp.int32, (16, half), 0)

    def scale_queries(g, coef):
        cols = slice(g * half, (g + 1) * half)
        c1, c2, _ = split3(coef)
        xt[0:nf, cols] = (qt[:, cols] * coef).astype(bf16)
        xt[nf:nf + 16, cols] = jnp.where(row == 0, c1, jnp.where(row == 1, c2, 0.0)).astype(bf16)

    def pushed(g, end, i):
        rows = slice(i * CHUNK, (i + 1) * CHUNK)
        cols = slice(g * half, end * half)
        return lax.dot_general(
            pt[rows, cols], xt[:, cols], (((1,), (1,)), ((), ())), preferred_element_type=f32
        )

    stores = [
        pltpu.make_async_copy(
            rg_ref.at[pl.ds(i * CHUNK, CHUNK)], rg_hbm.at[pl.ds(i * CHUNK, CHUNK)], rg_sem.at[i]
        )
        for i in range(nr // CHUNK)
    ]

    def finish(i, terms):
        rows = slice(i * CHUNK, (i + 1) * CHUNK)
        both = push[rows, :] + pushed(TURN[3], TURN[3] + 1, i)
        r = r_ref[rows, :]
        column = both[:, nf:nf + 1] + both[:, nf + 1:nf + 2]
        grad = (both[:, 0:nf] - r * column) * inv
        rg_ref[rows, :] = grad
        stores[i].start()
        return terms + jnp.sum(r * grad, axis=0, keepdims=True)

    per = half // TILE
    order = [g * per + i for g in TURN for i in range(per)]
    chunks = nr // CHUNK
    coefs = {}
    terms = jnp.zeros((1, nf), f32)

    def collect(g):
        coefs[g] = coefficients(g)
        return pull(g, coefs[g])

    bufs = (s0, s1)
    stage(order[0], s0, None, None)
    for i, t in enumerate(order):
        ahead = order[i + 1] if i + 1 < len(order) else None
        stage(ahead, bufs[(i + 1) % 2], t, bufs[i % 2])
        if (i + 1) % per:
            continue
        turn = (i + 1) // per - 1
        if turn == 0:
            pl.semaphore_wait(barrier, n - 1)
        spread_lse(TURN[turn])
        if turn >= 2:
            settle(TURN[turn - 2], 0)
        if turn >= 1:
            terms = terms + collect(TURN[turn - 1])
        if turn >= 2:
            for k in range(1, last):
                settle(TURN[turn - 2], k)

    early = TURN[:3]
    for g in early:
        scale_queries(g, coefs[g])
    for i in range(chunks):
        rows = slice(i * CHUNK, (i + 1) * CHUNK)
        push[rows, :] = pushed(0, 2, i) + pushed(3, 4, i)
        if i == 0:
            settle(early[2], 0)
    terms = (terms + collect(TURN[3])) * inv
    scale_queries(TURN[3], coefs[TURN[3]])
    for k in range(1, last):
        settle(early[2], k)
    for i in range(chunks):
        terms = finish(i, terms)
        if i == chunks // 2 - 1:
            settle(TURN[3], 0)
    term[...] = terms
    term_start, term_wait = all_to(term, term_rx, tm_send, tm_recv)
    term_start()
    for k in range(1, last):
        settle(TURN[3], k)
    for store in stores:
        store.wait()
    term_wait()
    summed = terms + jnp.sum(term_rx[...], axis=0)
    sg_ref[...] = -summed / sp - jnp.sum(cot_ref[...], axis=1, keepdims=True) / sp
    for j in range(1, GROUPS):
        final(j).wait()
    qg_ref[...] = (fin[group] + jnp.sum(fin_got[...], axis=0)) * inv


def hand_out(qg_in, rg_in, sg_in, qg_out, rg_out, sg_out, qg, rg, sg, load_sem, store_sem):
    rows = rg.shape[0]
    parts = [(qg_in, qg, qg_out), (sg_in, sg, sg_out)]
    for a in range(0, rows, CHUNK):
        piece = pl.ds(a, CHUNK)
        parts.append((rg_in.at[piece], rg.at[piece], rg_out.at[piece]))
    loads = [pltpu.make_async_copy(x, y, load_sem.at[i]) for i, (x, y, _) in enumerate(parts)]
    stores = [pltpu.make_async_copy(y, z, store_sem.at[i]) for i, (_, y, z) in enumerate(parts)]
    for load in loads:
        load.start()
    for load, store in zip(loads, stores):
        load.wait()
        store.start()
    for store in stores:
        store.wait()


def on_device(n, queries, references, query_ids, spread, cotangent):
    nq, nf = queries.shape
    nr = references.shape[0]
    own = nq // n
    half = nq // GROUPS
    f32, bf16 = jnp.float32, jnp.bfloat16
    last, _ = plan(n)
    shapes = layouts(n)
    dma = pltpu.SemaphoreType.DMA
    scratch = [
        pltpu.VMEM((nr, nf), f32),
        dma((nr // CHUNK,)),
        pltpu.VMEM((1, nq), jnp.int32),
        pltpu.VMEM((1, nf), f32),
        pltpu.VMEM((1, nq), f32),
        dma((3,)),
        pltpu.VMEM((4 * nf, nq), bf16),
        pltpu.VMEM((nr, 4 * nf), bf16),
        pltpu.VMEM((nf + 16, nr), bf16),
        pltpu.VMEM((nr, nq), bf16),
        pltpu.VMEM((nr, TILE), f32),
        pltpu.VMEM((nr, TILE), f32),
        pltpu.VMEM((1, nq), f32),
        pltpu.VMEM((nf + 16, nq), f32),
        pltpu.VMEM((nf, nq), f32),
        pltpu.VMEM((nf + 16, nq), bf16),
        pltpu.VMEM((nr, nf + 16), f32),
        pltpu.VMEM((GROUPS, own, nf), f32),
        pltpu.VMEM((GROUPS - 1, own, nf), f32),
        pltpu.VMEM((1, nf), f32),
        pltpu.VMEM((n - 1, 1, nf), f32),
    ]
    scratch += [pltpu.VMEM((1, half), f32)] * GROUPS
    scratch += [pltpu.VMEM((n - 1, 1, half), f32)] * GROUPS
    scratch += [pltpu.VMEM(shape + (own, nf), f32) for group in shapes for shape in group]
    scratch += [pltpu.VMEM((h, l, own, nf), f32) for group in shapes for h, _, l in group]
    scratch += [dma((1,))] * (2 * GROUPS) + [dma((last,))] * (2 * GROUPS)
    scratch += [dma((1,))] * 2 + [dma((GROUPS - 1,))] * 2
    vmem = pl.BlockSpec(memory_space=pltpu.VMEM)
    hbm = pl.BlockSpec(memory_space=pltpu.HBM)
    shapes_out = (
        jax.ShapeDtypeStruct((own, nf), f32),
        jax.ShapeDtypeStruct((nr, nf), f32),
        jax.ShapeDtypeStruct((1, nf), f32),
    )
    results = pl.pallas_call(
        functools.partial(kernel, n),
        out_shape=shapes_out,
        in_specs=[vmem, vmem, hbm, hbm, hbm],
        out_specs=(vmem, hbm, vmem),
        scratch_shapes=scratch,
        compiler_params=pltpu.CompilerParams(
            collective_id=0, has_side_effects=True, vmem_limit_bytes=62 * 2 ** 20
        ),
    )(queries, references, query_ids[None, :], spread[None, :], cotangent[None, :])
    query_grad, reference_grad, spread_grad = pl.pallas_call(
        hand_out,
        out_shape=shapes_out,
        in_specs=[pl.BlockSpec(memory_space=pl.ANY)] * 3,
        out_specs=(hbm, hbm, hbm),
        scratch_shapes=[pltpu.VMEM(x.shape, f32) for x in shapes_out]
        + [dma((2 + nr // CHUNK,))] * 2,
        compiler_params=pltpu.CompilerParams(vmem_limit_bytes=62 * 2 ** 20),
    )(*results)
    return query_grad, reference_grad, spread_grad[0]


def solution(mesh):
    placed = (P("parts", None), P(("parts", "ref"), None), P("parts"), P(), P("parts"))
    return jax.shard_map(
        functools.partial(on_device, mesh.shape["ref"]),
        mesh=mesh,
        in_specs=placed,
        out_specs=(P(("parts", "ref"), None), P(("parts", "ref"), None), P("parts")),
        check_vma=False,
    )
```

```python
import functools
import math

import jax
import jax.numpy as jnp
from jax import lax
from jax.experimental import pallas as pl
from jax.experimental.pallas import tpu as pltpu
from jax.sharding import PartitionSpec as P

LOG2E = math.log2(math.e)
TILE = 512
CHUNK = 512
SPAN = 1024


def split3(x):
    a = x.astype(jnp.bfloat16).astype(jnp.float32)
    b = (x - a).astype(jnp.bfloat16).astype(jnp.float32)
    c = (x - a - b).astype(jnp.bfloat16).astype(jnp.float32)
    return a, b, c


GROUPS = 4
TURN = (0, 3, 1, 2)


def plan(n):
    last = n.bit_length() - 3
    return last, [list(range(last))] * GROUPS


def layouts(n):
    last, orders = plan(n)
    shapes = []
    for order in orders:
        left = list(range(last))
        group = []
        for b in order:
            place = left.index(b)
            group.append((2 ** (len(left) - 1 - place), 2, 2 ** place))
            left.remove(b)
        shapes.append(group)
    return shapes


def kernel(
    n, q_ref, r_ref, ids_hbm, sp_hbm, cot_hbm, qg_ref, rg_hbm, sg_ref,
    rg_ref, rg_sem, ids_ref, sp_ref, cot_ref, in_sem,
    qat, ra, rta, pt, s0, s1, m_ref, ut, qt, xt, push, fin, fin_got, term, term_rx, *rest
):
    last, orders = plan(n)
    shapes = layouts(n)
    rest = list(rest)
    lse = [rest.pop(0) for _ in range(GROUPS)]
    lse_rx = [rest.pop(0) for _ in range(GROUPS)]
    acc = [[rest.pop(0) for _ in range(last)] for _ in range(GROUPS)]
    got = [[rest.pop(0) for _ in range(last)] for _ in range(GROUPS)]
    ls_send, ls_recv, rs_send, rs_recv = (rest[i * GROUPS:(i + 1) * GROUPS] for i in range(4))
    tm_send, tm_recv, fin_send, fin_recv = rest[4 * GROUPS:]
    nq, nf = q_ref.shape
    nr = r_ref.shape[0]
    own = nq // n
    half = nq // GROUPS
    f32, bf16 = jnp.float32, jnp.bfloat16
    me = lax.axis_index("ref")

    loads = [
        pltpu.make_async_copy(src, dst, in_sem.at[i])
        for i, (src, dst) in enumerate(((ids_hbm, ids_ref), (sp_hbm, sp_ref), (cot_hbm, cot_ref)))
    ]
    for load in loads:
        load.start()

    def peer_of(k):
        return lax.rem(me + k, n)

    barrier = pltpu.get_barrier_semaphore()

    def greet(k, carry):
        pl.semaphore_signal(
            barrier, inc=1, device_id={"ref": peer_of(k)}, device_id_type=pl.DeviceIdType.MESH
        )
        return carry

    lax.fori_loop(1, n, greet, 0)
    for load in loads:
        load.wait()

    sp = sp_ref[...]
    inv = 1.0 / (sp * sp)
    inv_col = jnp.transpose(jnp.broadcast_to(inv, (8, nf)))[:, :1]
    def prepare(t):
        rows = slice(t * TILE, (t + 1) * TILE)
        q_t = jnp.transpose(q_ref[rows, :])
        qt[:, rows] = q_t
        scaled = q_t * (inv_col * LOG2E)
        high = scaled.astype(bf16)
        low = (scaled - high.astype(f32)).astype(bf16)
        qat[0:nf, rows] = high
        qat[nf:2 * nf, rows] = low
        qat[2 * nf:3 * nf, rows] = high
        norm = -0.5 * jnp.sum(q_t * scaled, axis=0, keepdims=True)
        n1, n2, n3 = split3(norm)
        place = lax.broadcasted_iota(jnp.int32, (nf, TILE), 0)
        ext = jnp.where(place < 6, 1.0, 0.0)
        ext = jnp.where(place == 0, n1, ext)
        ext = jnp.where(place == 1, n2, ext)
        ext = jnp.where(place == 2, n3, ext)
        qat[3 * nf:4 * nf, rows] = ext.astype(bf16)
    for a in range(0, nr, TILE):
        rows = slice(a, a + TILE)
        r = r_ref[rows, :]
        high = r.astype(bf16)
        low = (r - high.astype(f32)).astype(bf16)
        ra[rows, 0:nf] = high
        ra[rows, nf:2 * nf] = high
        ra[rows, 2 * nf:3 * nf] = low
        norm = -0.5 * LOG2E * jnp.sum(r * r * inv, axis=1, keepdims=True)
        n1, n2, n3 = split3(norm)
        place = lax.broadcasted_iota(jnp.int32, (TILE, nf), 1)
        ext = jnp.where(place < 6, 1.0, 0.0)
        ext = jnp.where(place == 3, n1, ext)
        ext = jnp.where(place == 4, n2, ext)
        ext = jnp.where(place == 5, n3, ext)
        ra[rows, 3 * nf:4 * nf] = ext.astype(bf16)
        rta[0:nf, rows] = jnp.transpose(high)
    rta[nf:nf + 16, :] = jnp.ones((16, nr), bf16)

    start = me * nr

    def at(t):
        return pl.ds(pl.multiple_of(t * TILE, TILE), TILE)

    def score(t, s_ref, a, best):
        s = jnp.dot(ra[a:a + SPAN, :], qat[:, at(t)], preferred_element_type=f32)
        local = ids_ref[:, at(t)] - (start + a)
        hit = lax.broadcasted_iota(jnp.int32, (SPAN, TILE), 0) == local
        s = jnp.where(hit, -jnp.inf, s)
        s_ref[a:a + SPAN, :] = s
        top = jnp.max(s, axis=0, keepdims=True)
        return top if best is None else jnp.maximum(best, top)

    def weigh(t, s_ref, a, peak, total):
        p = jnp.exp2(s_ref[a:a + SPAN, :] - peak).astype(bf16)
        pt[a:a + SPAN, at(t)] = p
        part = jnp.dot(rta[:, a:a + SPAN], p, preferred_element_type=f32)
        return part if total is None else total + part

    def stage(ahead, s_ahead, t, s_now):
        best, total = None, None
        peak = None if t is None else m_ref[:, at(t)]
        for a in range(0, nr, SPAN):
            if ahead is not None:
                best = score(ahead, s_ahead, a, best)
            if t is not None:
                total = weigh(t, s_now, a, peak, total)
        if ahead is not None:
            m_ref[:, at(ahead)] = best
        if t is not None:
            ut[:, at(t)] = total

    def all_to(src, dst, send, recv):
        def copy(k):
            return pltpu.make_async_remote_copy(
                src_ref=src, dst_ref=dst.at[k - 1], send_sem=send.at[0], recv_sem=recv.at[0],
                device_id={"ref": peer_of(k)}, device_id_type=pl.DeviceIdType.MESH,
            )

        def begin(k, carry):
            copy(k).start()
            return carry

        def end():
            pltpu.make_async_copy(dst, dst, send.at[0]).wait()
            pltpu.make_async_copy(dst, dst, recv.at[0]).wait()

        return (lambda: lax.fori_loop(1, n, begin, 0)), end

    def spread_lse(g):
        cols = slice(g * half, (g + 1) * half)
        lse[g][...] = m_ref[:, cols] + jnp.log(ut[nf:nf + 1, cols]) * LOG2E
        all_to(lse[g], lse_rx[g], ls_send[g], ls_recv[g])[0]()

    def coefficients(g):
        cols = slice(g * half, (g + 1) * half)
        all_to(lse[g], lse_rx[g], ls_send[g], ls_recv[g])[1]()
        every = lse_rx[g][...]
        mine = lse[g][...]
        top = jnp.maximum(mine, jnp.max(every, axis=0))
        whole = jnp.exp2(mine - top) + jnp.sum(jnp.exp2(every - top[None]), axis=0)
        return cot_ref[:, cols] * jnp.exp2(m_ref[:, cols] - top) / whole

    def halving(g, i):
        size = 2 ** orders[g][i]
        bit = lax.rem(me // size, 2)
        return bit, pltpu.make_async_remote_copy(
            src_ref=acc[g][i].at[:, 1 - bit], dst_ref=got[g][i],
            send_sem=rs_send[g].at[i], recv_sem=rs_recv[g].at[i],
            device_id={"ref": me + (1 - 2 * bit) * size}, device_id_type=pl.DeviceIdType.MESH,
        )

    far = n // GROUPS
    group = lax.rem(me // far, GROUPS)

    def final(j):
        to = lax.rem(group + j, GROUPS)
        return pltpu.make_async_remote_copy(
            src_ref=fin.at[to], dst_ref=fin_got.at[j - 1],
            send_sem=fin_send.at[j - 1], recv_sem=fin_recv.at[j - 1],
            device_id={"ref": me + (to - group) * far}, device_id_type=pl.DeviceIdType.MESH,
        )

    def place_block(ref, shape, k, value):
        low = shape[2]
        ref[k // (2 * low), (k // low) % 2, k % low] = value

    def pull(g, coef):
        terms = jnp.zeros((1, nf), f32)
        for a in range(0, half, TILE):
            rows = slice(g * half + a, g * half + a + TILE)
            part = jnp.transpose(
                ut[0:nf, rows] * coef[:, a:a + TILE] - qt[:, rows] * (cot_ref[:, rows] * (1.0 / n))
            )
            terms = terms + jnp.sum(part * q_ref[rows, :], axis=0, keepdims=True)
            for b in range(0, TILE, own):
                place_block(acc[g][0], shapes[g][0], (a + b) // own, part[b:b + own])
        halving(g, 0)[1].start()
        return terms

    def settle(g, i):
        bit, copy = halving(g, i)
        copy.wait()
        high, _, low = shapes[g][i]
        for k in range(high * low):
            value = acc[g][i][k // low, bit, k % low] + got[g][i][k // low, k % low]
            if i + 1 < last:
                place_block(acc[g][i + 1], shapes[g][i + 1], k, value)
            else:
                fin[g] = value
        if i + 1 < last:
            halving(g, i + 1)[1].start()
        else:
            for j in range(1, GROUPS):
                pl.when(group == (g - j) % GROUPS)(final(j).start)

    row = lax.broadcasted_iota(jnp.int32, (16, half), 0)

    def scale_queries(g, coef):
        cols = slice(g * half, (g + 1) * half)
        c1, c2, _ = split3(coef)
        xt[0:nf, cols] = (qt[:, cols] * coef).astype(bf16)
        xt[nf:nf + 16, cols] = jnp.where(row == 0, c1, jnp.where(row == 1, c2, 0.0)).astype(bf16)

    def pushed(g, end, i):
        rows = slice(i * CHUNK, (i + 1) * CHUNK)
        cols = slice(g * half, end * half)
        return lax.dot_general(
            pt[rows, cols], xt[:, cols], (((1,), (1,)), ((), ())), preferred_element_type=f32
        )

    stores = [
        pltpu.make_async_copy(
            rg_ref.at[pl.ds(i * CHUNK, CHUNK)], rg_hbm.at[pl.ds(i * CHUNK, CHUNK)], rg_sem.at[i]
        )
        for i in range(nr // CHUNK)
    ]

    def finish(i, terms):
        rows = slice(i * CHUNK, (i + 1) * CHUNK)
        both = push[rows, :] + pushed(TURN[3], TURN[3] + 1, i)
        r = r_ref[rows, :]
        column = both[:, nf:nf + 1] + both[:, nf + 1:nf + 2]
        grad = (both[:, 0:nf] - r * column) * inv
        rg_ref[rows, :] = grad
        stores[i].start()
        return terms + jnp.sum(r * grad, axis=0, keepdims=True)

    per = half // TILE
    order = [g * per + i for g in TURN for i in range(per)]
    chunks = nr // CHUNK
    coefs = {}
    terms = jnp.zeros((1, nf), f32)

    def collect(g):
        coefs[g] = coefficients(g)
        return pull(g, coefs[g])

    bufs = (s0, s1)
    prepare(order[0])
    stage(order[0], s0, None, None)
    prepare(order[1])
    for i, t in enumerate(order):
        ahead = order[i + 1] if i + 1 < len(order) else None
        if i + 2 < len(order):
            prepare(order[i + 2])
        stage(ahead, bufs[(i + 1) % 2], t, bufs[i % 2])
        if (i + 1) % per:
            continue
        turn = (i + 1) // per - 1
        if turn == 0:
            pl.semaphore_wait(barrier, n - 1)
        spread_lse(TURN[turn])
        if turn >= 2:
            settle(TURN[turn - 2], 0)
        if turn >= 1:
            terms = terms + collect(TURN[turn - 1])
        if turn >= 2:
            for k in range(1, last):
                settle(TURN[turn - 2], k)

    early = TURN[:3]
    for g in early:
        scale_queries(g, coefs[g])
    for i in range(chunks):
        rows = slice(i * CHUNK, (i + 1) * CHUNK)
        push[rows, :] = pushed(0, 2, i) + pushed(3, 4, i)
        if i == 0:
            settle(early[2], 0)
    terms = (terms + collect(TURN[3])) * inv
    scale_queries(TURN[3], coefs[TURN[3]])
    for k in range(1, last):
        settle(early[2], k)
    for i in range(chunks):
        terms = finish(i, terms)
        if i == chunks // 2 - 1:
            settle(TURN[3], 0)
    term[...] = terms
    term_start, term_wait = all_to(term, term_rx, tm_send, tm_recv)
    term_start()
    for k in range(1, last):
        settle(TURN[3], k)
    for store in stores:
        store.wait()
    term_wait()
    summed = terms + jnp.sum(term_rx[...], axis=0)
    sg_ref[...] = -summed / sp - jnp.sum(cot_ref[...], axis=1, keepdims=True) / sp
    for j in range(1, GROUPS):
        final(j).wait()
    qg_ref[...] = (fin[group] + jnp.sum(fin_got[...], axis=0)) * inv


def hand_out(qg_in, rg_in, sg_in, qg_out, rg_out, sg_out, qg, rg, sg, load_sem, store_sem):
    rows = rg.shape[0]
    parts = [(qg_in, qg, qg_out), (sg_in, sg, sg_out)]
    for a in range(0, rows, CHUNK):
        piece = pl.ds(a, CHUNK)
        parts.append((rg_in.at[piece], rg.at[piece], rg_out.at[piece]))
    loads = [pltpu.make_async_copy(x, y, load_sem.at[i]) for i, (x, y, _) in enumerate(parts)]
    stores = [pltpu.make_async_copy(y, z, store_sem.at[i]) for i, (_, y, z) in enumerate(parts)]
    for load in loads:
        load.start()
    for load, store in zip(loads, stores):
        load.wait()
        store.start()
    for store in stores:
        store.wait()


def on_device(n, queries, references, query_ids, spread, cotangent):
    nq, nf = queries.shape
    nr = references.shape[0]
    own = nq // n
    half = nq // GROUPS
    f32, bf16 = jnp.float32, jnp.bfloat16
    last, _ = plan(n)
    shapes = layouts(n)
    dma = pltpu.SemaphoreType.DMA
    scratch = [
        pltpu.VMEM((nr, nf), f32),
        dma((nr // CHUNK,)),
        pltpu.VMEM((1, nq), jnp.int32),
        pltpu.VMEM((1, nf), f32),
        pltpu.VMEM((1, nq), f32),
        dma((3,)),
        pltpu.VMEM((4 * nf, nq), bf16),
        pltpu.VMEM((nr, 4 * nf), bf16),
        pltpu.VMEM((nf + 16, nr), bf16),
        pltpu.VMEM((nr, nq), bf16),
        pltpu.VMEM((nr, TILE), f32),
        pltpu.VMEM((nr, TILE), f32),
        pltpu.VMEM((1, nq), f32),
        pltpu.VMEM((nf + 16, nq), f32),
        pltpu.VMEM((nf, nq), f32),
        pltpu.VMEM((nf + 16, nq), bf16),
        pltpu.VMEM((nr, nf + 16), f32),
        pltpu.VMEM((GROUPS, own, nf), f32),
        pltpu.VMEM((GROUPS - 1, own, nf), f32),
        pltpu.VMEM((1, nf), f32),
        pltpu.VMEM((n - 1, 1, nf), f32),
    ]
    scratch += [pltpu.VMEM((1, half), f32)] * GROUPS
    scratch += [pltpu.VMEM((n - 1, 1, half), f32)] * GROUPS
    scratch += [pltpu.VMEM(shape + (own, nf), f32) for group in shapes for shape in group]
    scratch += [pltpu.VMEM((h, l, own, nf), f32) for group in shapes for h, _, l in group]
    scratch += [dma((1,))] * (2 * GROUPS) + [dma((last,))] * (2 * GROUPS)
    scratch += [dma((1,))] * 2 + [dma((GROUPS - 1,))] * 2
    vmem = pl.BlockSpec(memory_space=pltpu.VMEM)
    hbm = pl.BlockSpec(memory_space=pltpu.HBM)
    shapes_out = (
        jax.ShapeDtypeStruct((own, nf), f32),
        jax.ShapeDtypeStruct((nr, nf), f32),
        jax.ShapeDtypeStruct((1, nf), f32),
    )
    results = pl.pallas_call(
        functools.partial(kernel, n),
        out_shape=shapes_out,
        in_specs=[vmem, vmem, hbm, hbm, hbm],
        out_specs=(vmem, hbm, vmem),
        scratch_shapes=scratch,
        compiler_params=pltpu.CompilerParams(
            collective_id=0, has_side_effects=True, vmem_limit_bytes=62 * 2 ** 20
        ),
    )(queries, references, query_ids[None, :], spread[None, :], cotangent[None, :])
    query_grad, reference_grad, spread_grad = pl.pallas_call(
        hand_out,
        out_shape=shapes_out,
        in_specs=[pl.BlockSpec(memory_space=pl.ANY)] * 3,
        out_specs=(hbm, hbm, hbm),
        scratch_shapes=[pltpu.VMEM(x.shape, f32) for x in shapes_out]
        + [dma((2 + nr // CHUNK,))] * 2,
        compiler_params=pltpu.CompilerParams(vmem_limit_bytes=62 * 2 ** 20),
    )(*results)
    return query_grad, reference_grad, spread_grad[0]


def solution(mesh):
    placed = (P("parts", None), P(("parts", "ref"), None), P("parts"), P(), P("parts"))
    return jax.shard_map(
        functools.partial(on_device, mesh.shape["ref"]),
        mesh=mesh,
        in_specs=placed,
        out_specs=(P(("parts", "ref"), None), P(("parts", "ref"), None), P("parts")),
        check_vma=False,
    )
```
